128 devices in a mesh: seq: 16 (over z, y), head: 8 (over x, core).
Axes of the slice: x: 4, y: 4, z: 4, core: 2. Of those that a mesh axis runs over, the one named last changes fastest.
Arguments:
- query_rows: bfloat16 [32768, 3072], P(('seq', 'head')), may hold values from -32 to 32
- key_rows: bfloat16 [32768, 3072], P(('seq', 'head')), may hold values from -32 to 32
- value_rows: bfloat16 [32768, 3072], P(('seq', 'head')), may hold values from -6 to 6
- query_cluster: int32 [24, 32768], P('head', 'seq'), may hold values from 0 to 255, as said below
- key_cluster: int32 [24, 32768], P('head', 'seq'), may hold values from 0 to 255, as said below
- cluster_pairs: int32 [24, 256, 16], P('head'), may hold values from 0 to 255, as said below
Outputs:
- attended: bfloat16 [32768, 3072], P(('seq', 'head'))
The draws below stay inside these ranges and needn't reach their ends.
Inputs may be any that keep to these rules, and one draw needn't show every extreme that they name: `query_cluster`: for each head every cluster number names exactly 128 tokens. Cluster numbers form groups of 16 consecutive ones, numbered like the aligned blocks of 2048 token positions; for each head at most 192 tokens of one block lie in the clusters of one group, and some block and group reach it. `key_cluster`: likewise for key clusters: exactly 128 tokens a cluster, at most 192 tokens of one block in the clusters of one group, reached. `cluster_pairs`: each row names 16 different key clusters. For each head the rows of one group of 16 query clusters name at most 4 different key clusters of one group, and some pair of groups reaches it.
All inputs are finite; a program needn't handle non-finite values.
Results may differ from the reference program's by a relative error of at most 0.0047.
Values may be sent and summed in bfloat16 or wider, within the bound.
No kernel may reach another device: no remote copies, remote signals or barrier semaphores. Data moves between devices by JAX's collectives and lax.ppermute only.
A program may use at most 192 MiB of HBM per device.

```python
import math
import jax
import jax.numpy as jnp
from jax import lax

HEADS = 24
HDIM = 128
BLOCK = 128
PAIRS = 16
KCAP = 4
CL_DEV = 16
TOK_DEV = 2048
TOKENS = 32768
CLUSTERS = 256
N_SEQ = 16


def permute_tokens(subkey):
    return jax.random.permutation(subkey, TOK_DEV)


def permute_group(subkey):
    return jax.random.permutation(subkey, CL_DEV)


def permute_clusters(subkey):
    return jax.random.permutation(subkey, CLUSTERS)


def route_head(key):
    per_pair = TOK_DEV // N_SEQ
    keys = jax.random.split(key, 4)
    sigma = jax.random.permutation(keys[0], N_SEQ)
    columns = jnp.arange(N_SEQ)
    direct = (sigma[:, None] == columns[None, :]).astype(jnp.int32)
    beside = (((sigma + 1) % N_SEQ)[:, None] == columns[None, :]).astype(jnp.int32)
    spread = jax.random.randint(keys[1], (N_SEQ, N_SEQ), 0, per_pair // 8 + 1)
    first = sigma[0]
    after = (first + 1) % N_SEQ
    spread = spread.at[0, first].set(per_pair // 8).at[0, after].set(0)
    spread = spread.at[1, first].set(0).at[1, after].set(per_pair // 8)
    shifted_rows = jnp.roll(spread, -1, axis=0)
    wiggle = spread - jnp.roll(spread, -1, axis=1) - shifted_rows + jnp.roll(shifted_rows, -1, axis=1)
    counts = per_pair + wiggle + per_pair // 4 * (direct - beside)
    bounds = jnp.cumsum(counts, axis=1)
    ranks = jnp.arange(TOK_DEV)
    target_sorted = jnp.sum((ranks[None, :, None] >= bounds[:, None, :]).astype(jnp.int32), axis=-1)
    shuffles = jax.vmap(permute_tokens)(jax.random.split(keys[2], N_SEQ))
    target = jnp.take_along_axis(target_sorted, shuffles, axis=1).reshape(TOKENS)
    onehot = (target[:, None] == columns[None, :]).astype(jnp.int32)
    ordinal = jnp.sum((jnp.cumsum(onehot, axis=0) - onehot) * onehot, axis=1)
    inner = jax.vmap(permute_tokens)(jax.random.split(keys[3], N_SEQ))
    spot = inner[target, ordinal]
    return (target * CL_DEV + spot // BLOCK).astype(jnp.int32)


def pair_head(key):
    keys = jax.random.split(key, 4)
    counts = jax.random.randint(keys[0], (N_SEQ, N_SEQ), 2, KCAP + 1)
    offset = jax.random.randint(keys[1], (), 0, N_SEQ)
    lanes = jnp.arange(N_SEQ)
    counts = jnp.where(lanes[None, :] == (lanes[:, None] + offset) % N_SEQ, KCAP, counts)
    ranked = jax.vmap(permute_group)(jax.random.split(keys[2], N_SEQ * N_SEQ)).reshape(N_SEQ, N_SEQ, CL_DEV)
    chosen = (ranked < counts[:, :, None]).reshape(N_SEQ, CLUSTERS)
    shuffle = jax.vmap(permute_clusters)(jax.random.split(keys[3], N_SEQ))
    sort_score = jnp.where(chosen, 0, CLUSTERS) + shuffle
    union = jnp.argsort(sort_score, axis=1).astype(jnp.int32)
    union_size = jnp.sum(chosen.astype(jnp.int32), axis=1)
    flat_slots = jnp.arange(CL_DEV * PAIRS).reshape(CL_DEV, PAIRS)
    position_in = flat_slots[None, :, :] % union_size[:, None, None]
    picked = union[lanes[:, None, None], position_in]
    return picked.reshape(CLUSTERS, PAIRS).astype(jnp.int32)


def draw_query_rows(key, part):
    key = jax.random.fold_in(key, 21)
    base = jnp.clip(jax.random.normal(key, (TOKENS, HEADS, HDIM), jnp.float32), -6.0, 6.0)
    return base.reshape(TOKENS, HEADS * HDIM).astype(jnp.bfloat16)


def draw_key_rows(key, part):
    key = jax.random.fold_in(key, 22)
    base = jnp.clip(jax.random.normal(key, (TOKENS, HEADS, HDIM), jnp.float32), -6.0, 6.0)
    return base.reshape(TOKENS, HEADS * HDIM).astype(jnp.bfloat16)


def draw_query_cluster(key, part):
    key = jax.random.fold_in(key, 11)
    return jax.vmap(route_head)(jax.random.split(key, HEADS))


def draw_key_cluster(key, part):
    key = jax.random.fold_in(key, 12)
    return jax.vmap(route_head)(jax.random.split(key, HEADS))


def draw_cluster_pairs(key, part):
    key = jax.random.fold_in(key, 13)
    return jax.vmap(pair_head)(jax.random.split(key, HEADS))


def level_of(stream_key, extent, cuts, least, high):
    gain = 1.0
    for dim, parts in cuts:
        heights = jax.random.uniform(jax.random.fold_in(jax.random.fold_in(stream_key, 6), dim), (parts,), jnp.float32, least / len(cuts), high / len(cuts))
        gain = gain * jnp.repeat(jnp.exp(heights), extent[dim] // parts).reshape((-1,) + (1,) * (len(extent) - 1 - dim))
    return gain


def bell_draw(own_key, extent, width, bound, pieces=(), held_as=jnp.bfloat16):
    values = jax.random.normal(own_key, extent, jnp.float32) * width
    if len(pieces) > 0:
        values = level_of(own_key, extent, pieces, -0.22, 0.18) * values
    return jnp.clip(values, min=-bound, max=bound).astype(held_as)


def setup_inputs(seed: int = 0) -> dict:
    splits = jax.random.split(jax.random.key(seed), 7)
    query_rows = draw_query_rows(jax.random.fold_in(splits[6], 71), 0)
    key_rows = draw_key_rows(jax.random.fold_in(splits[6], 71), 0)
    value_rows = bell_draw(splits[2], (TOKENS, HEADS * HDIM), 1.0, 6.0, ((0, 128),))
    query_cluster = draw_query_cluster(jax.random.fold_in(splits[6], 71), 0)
    key_cluster = draw_key_cluster(jax.random.fold_in(splits[6], 71), 0)
    cluster_pairs = draw_cluster_pairs(jax.random.fold_in(splits[6], 71), 0)
    return dict(query_rows=query_rows, key_rows=key_rows, value_rows=value_rows, query_cluster=query_cluster, key_cluster=key_cluster, cluster_pairs=cluster_pairs)


def attend_head(packed):
    query_head, key_head, value_head, query_ids, key_ids, pair_rows = packed
    query_order = jnp.argsort(query_ids, stable=True)
    key_order = jnp.argsort(key_ids, stable=True)
    query_blocks = query_head[query_order].reshape(CLUSTERS, BLOCK, HDIM)
    key_blocks = key_head[key_order].reshape(CLUSTERS, BLOCK, HDIM)
    value_blocks = value_head[key_order].reshape(CLUSTERS, BLOCK, HDIM)
    score_scale = 1.0 / math.sqrt(HDIM)

    def one_cluster(item):
        block_rows, chosen = item
        keys_used = key_blocks[chosen].reshape(PAIRS * BLOCK, HDIM)
        values_used = value_blocks[chosen].reshape(PAIRS * BLOCK, HDIM)
        scores = jnp.dot(block_rows, keys_used.T, preferred_element_type=jnp.float32) * score_scale
        row_max = lax.optimization_barrier(jnp.max(scores, axis=1, keepdims=True))
        weights = jnp.exp(scores - row_max)
        total = lax.optimization_barrier(jnp.sum(weights, axis=1, keepdims=True))
        mixed = jnp.dot(weights.astype(jnp.bfloat16), values_used, preferred_element_type=jnp.float32)
        return (mixed / total).astype(jnp.bfloat16)
    outputs = lax.map(one_cluster, (query_blocks, pair_rows))
    placed = jnp.zeros((TOKENS, HDIM), outputs.dtype)
    return placed.at[query_order].set(outputs.reshape(TOKENS, HDIM))

def reference(query_rows, key_rows, value_rows, query_cluster, key_cluster, cluster_pairs):

    def by_head(rows):
        return rows.reshape(TOKENS, HEADS, HDIM).transpose(1, 0, 2)
    results = lax.map(attend_head, (by_head(query_rows), by_head(key_rows), by_head(value_rows), query_cluster, key_cluster, cluster_pairs))
    return results.transpose(1, 0, 2).reshape(TOKENS, HEADS * HDIM)
```

```python
import functools
import math

import jax
import jax.numpy as jnp
from jax import lax
from jax.experimental import pallas as pl
from jax.experimental.pallas import tpu as pltpu
from jax.sharding import PartitionSpec as P

BLOCK = 128
PAIRS = 16
KCAP = 4
LANES = 128
META = 16
VMEM_LIMIT = 56 * 1024 * 1024
BF16 = jnp.bfloat16
F32 = jnp.float32
I32 = jnp.int32


def dot(left, right):
    return jnp.dot(left, right, preferred_element_type=F32)


def iota(shape, dim):
    return lax.broadcasted_iota(I32, shape, dim)


def params():
    return pltpu.CompilerParams(vmem_limit_bytes=VMEM_LIMIT)


def slot_kernel(ids_ref, slot_ref, count_ref, *, groups, owned, capacity):
    clusters = groups * owned
    chunks = ids_ref.shape[1]
    row = iota((clusters, LANES), 0)
    lane = iota((clusters, LANES), 1)
    before = iota((LANES, 2 * LANES), 0)
    after = iota((LANES, 2 * LANES), 1)
    running = ((after >= LANES) | (before <= after)).astype(BF16)
    every = jnp.ones((LANES, LANES), BF16)
    counts = jnp.zeros((clusters, LANES), F32)
    for chunk in range(chunks):
        hit = (ids_ref[0, chunk : chunk + 1, :] == row).astype(BF16)
        counts = counts + dot(hit, every)
    first = iota((clusters, clusters), 0)
    second = iota((clusters, clusters), 1)
    inside = ((second < first) & (second // owned == first // owned)).astype(BF16)
    carry = dot(inside, counts.astype(BF16)) + ((row // owned) * capacity - 1).astype(F32)
    own = jnp.where(lane == row % owned, counts, 0.0).astype(BF16)
    of_group = (iota((groups, clusters), 0) == iota((groups, clusters), 1) // owned).astype(BF16)
    count_ref[0] = dot(of_group, own)
    for chunk in range(chunks):
        match = ids_ref[0, chunk : chunk + 1, :] == row
        sums = dot(match.astype(BF16), running)
        picked = jnp.where(match, sums[:, :LANES] + carry, 0.0)
        slot_ref[0, chunk : chunk + 1, :] = jnp.sum(picked, axis=0, keepdims=True).astype(I32)
        carry = carry + sums[:, LANES:]


def spread(index, rows, store, slots, step):
    flat = jnp.concatenate([index[i : i + 1, :] for i in range(index.shape[0])], axis=1)
    count = flat.shape[1]
    within = iota((step, count), 0)

    def body(i, carry):
        onehot = (flat - i * step == within).astype(BF16)
        store(i, dot(onehot, rows).astype(BF16))
        return carry

    lax.fori_loop(0, slots // step, body, 0)


def collect(index, packed, wide_ref, store, step):
    turned = index.astype(F32).T
    chunks = index.shape[0]
    for i in range(chunks):
        wide_ref[i * LANES : (i + 1) * LANES, :] = jnp.broadcast_to(
            turned[:, i : i + 1], (LANES, LANES)
        ).astype(I32)
    lane = iota((step, LANES), 1)
    tiles = packed.shape[0] // LANES

    def body(i, carry):
        wide = wide_ref[pl.ds(pl.multiple_of(i * step, step), step), :] - lane
        onehot = jnp.concatenate([(wide == t * LANES).astype(BF16) for t in range(tiles)], axis=1)
        store(i, dot(onehot, packed).astype(BF16))
        return carry

    lax.fori_loop(0, chunks * LANES // step, body, 0)


def pack_kv_kernel(slot_ref, key_count_ref, query_count_ref, key_ref, value_ref, out_ref):
    groups, _, rows, _ = out_ref.shape
    capacity = rows - META
    tokens = key_ref.shape[0] * key_ref.shape[2]
    keys = key_ref[:, 0].reshape(tokens, LANES)
    values = value_ref[:, 0].reshape(tokens, LANES)

    def store(i, block):
        out_ref[pl.ds(2 * i, 2), 0, :capacity, :] = block.reshape(2, capacity, 2 * LANES)

    both = jnp.concatenate([keys, values], axis=1)
    spread(slot_ref[0], both, store, groups * capacity, 2 * capacity)
    for group in range(groups):
        key_count = jnp.broadcast_to(key_count_ref[0, group : group + 1, :], (META, LANES))
        query_count = jnp.broadcast_to(query_count_ref[0, group : group + 1, :], (META, LANES))
        out_ref[group, 0, capacity:, :LANES] = key_count.astype(BF16)
        out_ref[group, 0, capacity:, LANES:] = query_count.astype(BF16)


def pack_q_kernel(slot_ref, query_ref, out_ref):
    groups, _, capacity, _ = out_ref.shape
    tokens = query_ref.shape[0] * query_ref.shape[1]

    def store(i, block):
        out_ref[pl.ds(2 * i, 2), 0] = block.reshape(2, capacity, LANES)

    queries = query_ref[...].reshape(tokens, LANES)
    spread(slot_ref[0], queries, store, groups * capacity, 2 * capacity)


def sources(counts, capacity):
    groups = counts.shape[0]
    padded = jnp.concatenate([counts, jnp.zeros((LANES - groups, LANES), F32)], axis=0).astype(BF16)
    row = iota((LANES, LANES), 0)
    col = iota((LANES, LANES), 1)
    below = dot((col < row).astype(BF16), padded)
    offset = dot(padded, (row < col).astype(BF16))
    start = (row * capacity).astype(F32) + offset - below
    below_t = below.T[:groups]
    start_t = start.T[:groups]
    place = iota((groups, LANES), 1).astype(F32)
    found = jnp.broadcast_to(start_t[:, 0:1], (groups, LANES))
    for source in range(1, groups):
        found = jnp.where(below_t[:, source : source + 1] <= place, start_t[:, source : source + 1], found)
    return (found + place).astype(I32)


def unpack_kv_kernel(pick_ref, in_ref, out_ref, query_source_ref, wide_ref, sorted_ref, *, first):
    head = pl.program_id(0) + first
    groups, _, rows, _ = in_ref.shape
    capacity = rows - META
    counts = in_ref[:, 0, capacity:, :].astype(F32)
    counts = jnp.max(counts, axis=1)
    query_source_ref[0] = sources(counts[:, LANES:], capacity)
    packed = in_ref[:, 0, :capacity, :].reshape(groups * capacity, 2 * LANES)

    def store(i, block):
        sorted_ref[pl.ds(4 * i, 4)] = block.reshape(4, BLOCK, 2 * LANES)

    collect(sources(counts[:, :LANES], capacity), packed, wide_ref, store, 4 * BLOCK)

    def copy(i, carry):
        for j in range(KCAP):
            out_ref[i, 0, j] = sorted_ref[pick_ref[head, i, j]]
        return carry

    lax.fori_loop(0, groups, copy, 0)


def unpack_q_kernel(index_ref, in_ref, out_ref, wide_ref):
    groups, _, capacity, _ = in_ref.shape
    packed = in_ref[:, 0].reshape(groups * capacity, LANES)
    step = 4 * BLOCK

    def store(i, block):
        out_ref[0, pl.ds(pl.multiple_of(i * step, step), step), :] = block

    collect(index_ref[0], packed, wide_ref, store, step)


def final_kernel(index_ref, in_ref, out_ref, wide_ref):
    groups, _, capacity, _ = in_ref.shape
    packed = in_ref[:, 0].reshape(groups * capacity, LANES)
    part = out_ref.shape[1]

    def store(i, block):
        out_ref[pl.ds(2 * i, 2)] = block.reshape(2, part, LANES)

    collect(index_ref[0], packed, wide_ref, store, 2 * part)


def attend_kernel(fetch_ref, index_ref, query_ref, recv_ref, out_ref, attended_ref, *, first):
    head = pl.program_id(0) + first
    groups, _, capacity, _ = out_ref.shape
    owned = query_ref.shape[1] // BLOCK
    scale = 1.0 / math.sqrt(LANES)

    def one(cluster):
        rows = pl.ds(pl.multiple_of(cluster * BLOCK, BLOCK), BLOCK)
        queries = query_ref[0, rows, :]
        blocks = []
        for pair in range(PAIRS):
            at = fetch_ref[head, cluster, pair]
            blocks.append((at // KCAP, at % KCAP))
        keys = jnp.concatenate([recv_ref[b, 0, j, :, :LANES] for b, j in blocks], axis=0)
        values = jnp.concatenate([recv_ref[b, 0, j, :, LANES:] for b, j in blocks], axis=0)
        scores = lax.dot_general(
            queries, keys, (((1,), (1,)), ((), ())), preferred_element_type=F32
        )
        scores = scores * scale
        weights = jnp.exp(scores - jnp.max(scores, axis=1, keepdims=True))
        total = jnp.sum(weights, axis=1, keepdims=True)
        mixed = dot(weights.astype(BF16), values)
        attended_ref[rows, :] = (mixed / total).astype(BF16)

    def body(i, carry):
        one(2 * i)
        one(2 * i + 1)
        return carry

    lax.fori_loop(0, owned // 2, body, 0)

    def store(i, block):
        out_ref[pl.ds(2 * i, 2), 0] = block.reshape(2, capacity, LANES)

    spread(index_ref[0], attended_ref[...], store, groups * capacity, 2 * capacity)


def shape_of(shape, dtype):
    return jax.ShapeDtypeStruct(shape, dtype)


def cost(flops, moved, exps=0):
    return pl.CostEstimate(flops=int(flops), bytes_accessed=int(moved), transcendentals=int(exps))


def exchange(array, axis):
    return lax.all_to_all(array, axis, split_axis=0, concat_axis=0, tiled=True)


def tables(cluster_pairs, my_index, groups):
    heads, clusters, _ = cluster_pairs.shape
    owned = clusters // groups
    by_group = cluster_pairs.reshape(heads, groups, owned * PAIRS)
    local = jnp.arange(owned, dtype=I32)
    earlier = (local[:, None] < local[None, :]).astype(F32)
    needed = jnp.any(by_group[:, :, None, :] == (my_index * owned + local)[None, None, :, None], axis=3)
    order = jnp.einsum("hac,cd->had", needed.astype(F32), earlier).astype(I32)
    hits = needed[:, :, None, :] & (order[:, :, None, :] == jnp.arange(KCAP, dtype=I32)[:, None])
    pick = jnp.sum(jnp.where(hits, local, 0), axis=3)
    own = lax.dynamic_index_in_dim(by_group, my_index, 1, keepdims=False)
    every = jnp.arange(clusters, dtype=I32)
    same = own[:, :, None] == every
    wanted = jnp.any(same, axis=1).reshape(heads, groups, owned)
    rank = jnp.einsum("hac,cd->had", wanted.astype(F32), earlier).astype(I32)
    position = (rank + jnp.arange(groups, dtype=I32)[None, :, None] * KCAP).reshape(heads, 1, clusters)
    fetch = jnp.sum(jnp.where(same, position, 0), axis=2)
    return pick, fetch.reshape(heads, owned, PAIRS)


def per_device(query_rows, key_rows, value_rows, query_cluster, key_cluster, cluster_pairs):
    heads, tokens = query_cluster.shape
    groups = lax.axis_size("seq")
    parts = lax.axis_size("head")
    my_index = lax.axis_index("seq")
    clusters = cluster_pairs.shape[1]
    owned = clusters // groups
    capacity = 3 * tokens // (2 * groups)
    slots = groups * capacity
    part = tokens // parts
    width = heads * LANES
    chunks = tokens // LANES

    def by_part(rows):
        return rows.reshape(part, parts, width).transpose(1, 0, 2)

    kv_sent = jnp.stack([by_part(key_rows), by_part(value_rows)], axis=1)
    kv_tok = exchange(kv_sent, "head")
    q_tok = exchange(by_part(query_rows), "head")

    ids = jnp.concatenate([query_cluster, key_cluster], axis=0).reshape(2 * heads, chunks, LANES)
    slot, count = pl.pallas_call(
        functools.partial(slot_kernel, groups=groups, owned=owned, capacity=capacity),
        grid=(2 * heads,),
        in_specs=[pl.BlockSpec((1, chunks, LANES), lambda h: (h, 0, 0))],
        out_specs=[
            pl.BlockSpec((1, chunks, LANES), lambda h: (h, 0, 0)),
            pl.BlockSpec((1, groups, LANES), lambda h: (h, 0, 0)),
        ],
        out_shape=[
            shape_of((2 * heads, chunks, LANES), I32),
            shape_of((2 * heads, groups, LANES), F32),
        ],
        compiler_params=params(),
        cost_estimate=cost(2e9 * heads, 1e6),
        name="slots",
    )(ids)
    pick, fetch = tables(cluster_pairs, my_index, groups)

    kv_packed = pl.pallas_call(
        pack_kv_kernel,
        grid=(heads,),
        in_specs=[
            pl.BlockSpec((1, chunks, LANES), lambda h: (h + heads, 0, 0)),
            pl.BlockSpec((1, groups, LANES), lambda h: (h + heads, 0, 0)),
            pl.BlockSpec((1, groups, LANES), lambda h: (h, 0, 0)),
            pl.BlockSpec((parts, 1, part, LANES), lambda h: (0, 0, 0, h)),
            pl.BlockSpec((parts, 1, part, LANES), lambda h: (0, 1, 0, h)),
        ],
        out_specs=pl.BlockSpec((groups, 1, capacity + META, 2 * LANES), lambda h: (0, h, 0, 0)),
        out_shape=shape_of((groups, heads, capacity + META, 2 * LANES), BF16),
        compiler_params=params(),
        cost_estimate=cost(heads * 4.0 * slots * tokens * LANES, 8e6),
        name="pack_kv",
    )(slot, count, count, kv_tok, kv_tok)
    kv_recv = exchange(kv_packed, "seq")

    q_packed = pl.pallas_call(
        pack_q_kernel,
        grid=(heads,),
        in_specs=[
            pl.BlockSpec((1, chunks, LANES), lambda h: (h, 0, 0)),
            pl.BlockSpec((parts, part, LANES), lambda h: (0, 0, h)),
        ],
        out_specs=pl.BlockSpec((groups, 1, capacity, LANES), lambda h: (0, h, 0, 0)),
        out_shape=shape_of((groups, heads, capacity, LANES), BF16),
        compiler_params=params(),
        cost_estimate=cost(heads * 4.0 * slots * tokens * LANES, 4e6),
        name="pack_q",
    )(slot, q_tok)
    q_recv = exchange(q_packed, "seq")

    def unpack_kv(first, count_heads):
        return pl.pallas_call(
            functools.partial(unpack_kv_kernel, first=first),
            grid_spec=pltpu.PrefetchScalarGridSpec(
                num_scalar_prefetch=1,
                grid=(count_heads,),
                in_specs=[
                    pl.BlockSpec(
                        (groups, 1, capacity + META, 2 * LANES), lambda h, pick: (0, h + first, 0, 0)
                    ),
                ],
                out_specs=[
                    pl.BlockSpec(
                        (groups, 1, KCAP, BLOCK, 2 * LANES), lambda h, pick: (0, h, 0, 0, 0)
                    ),
                    pl.BlockSpec((1, owned, BLOCK), lambda h, pick: (h, 0, 0)),
                ],
                scratch_shapes=[
                    pltpu.VMEM((owned * BLOCK, LANES), I32),
                    pltpu.VMEM((owned, BLOCK, 2 * LANES), BF16),
                ],
            ),
            out_shape=[
                shape_of((groups, count_heads, KCAP, BLOCK, 2 * LANES), BF16),
                shape_of((count_heads, owned, BLOCK), I32),
            ],
            compiler_params=params(),
            cost_estimate=cost(count_heads * 4.0 * slots * tokens * LANES, count_heads * 6e6),
            name=f"unpack_kv_{first}",
        )(pick, kv_recv)

    splits = ((0, 1), (1, heads - 1))
    received = []
    indices = []
    for first, count_heads in splits:
        sent, index = unpack_kv(first, count_heads)
        indices.append(index)
        received.append(exchange(sent, "seq"))
    index = jnp.concatenate(indices, axis=0)

    q_sorted = pl.pallas_call(
        unpack_q_kernel,
        grid=(heads,),
        in_specs=[
            pl.BlockSpec((1, owned, BLOCK), lambda h: (h, 0, 0)),
            pl.BlockSpec((groups, 1, capacity, LANES), lambda h: (0, h, 0, 0)),
        ],
        out_specs=pl.BlockSpec((1, owned * BLOCK, LANES), lambda h: (h, 0, 0)),
        out_shape=shape_of((heads, owned * BLOCK, LANES), BF16),
        scratch_shapes=[pltpu.VMEM((owned * BLOCK, LANES), I32)],
        compiler_params=params(),
        cost_estimate=cost(heads * 4.0 * slots * tokens * LANES, 4e6),
        name="unpack_q",
    )(index, q_recv)

    replies = []
    for (first, count_heads), recv in zip(splits, received, strict=True):
        replies.append(
            pl.pallas_call(
                functools.partial(attend_kernel, first=first),
                grid_spec=pltpu.PrefetchScalarGridSpec(
                    num_scalar_prefetch=1,
                    grid=(count_heads,),
                    in_specs=[
                        pl.BlockSpec((1, owned, BLOCK), lambda h, fetch, first=first: (h + first, 0, 0)),
                        pl.BlockSpec(
                            (1, owned * BLOCK, LANES), lambda h, fetch, first=first: (h + first, 0, 0)
                        ),
                        pl.BlockSpec(
                            (groups, 1, KCAP, BLOCK, 2 * LANES), lambda h, fetch: (0, h, 0, 0, 0)
                        ),
                    ],
                    out_specs=pl.BlockSpec(
                        (groups, 1, capacity, LANES), lambda h, fetch: (0, h, 0, 0)
                    ),
                    scratch_shapes=[pltpu.VMEM((owned * BLOCK, LANES), BF16)],
                ),
                out_shape=shape_of((groups, count_heads, capacity, LANES), BF16),
                compiler_params=params(),
                cost_estimate=cost(
                    count_heads * 4.0 * owned * BLOCK * PAIRS * BLOCK * LANES,
                    count_heads * 6e6,
                    count_heads * owned * BLOCK * PAIRS * BLOCK,
                ),
                name=f"attend_{first}",
            )(fetch, index, q_sorted, recv)
        )
    reply = jnp.concatenate(replies, axis=1)
    returned = exchange(reply, "seq")
    token_rows = pl.pallas_call(
        final_kernel,
        grid=(heads,),
        in_specs=[
            pl.BlockSpec((1, chunks, LANES), lambda h: (h, 0, 0)),
            pl.BlockSpec((groups, 1, capacity, LANES), lambda h: (0, h, 0, 0)),
        ],
        out_specs=pl.BlockSpec((parts, part, LANES), lambda h: (0, 0, h)),
        out_shape=shape_of((parts, part, width), BF16),
        scratch_shapes=[pltpu.VMEM((tokens, LANES), I32)],
        compiler_params=params(),
        cost_estimate=cost(heads * 4.0 * slots * tokens * LANES, 4e6),
        name="final",
    )(slot, returned)
    rows = exchange(token_rows, "head")
    return rows.transpose(1, 0, 2).reshape(part, parts * width)


def solution(mesh):
    in_specs = (
        P(("seq", "head"), None),
        P(("seq", "head"), None),
        P(("seq", "head"), None),
        P("head", "seq"),
        P("head", "seq"),
        P("head", None, None),
    )
    out_specs = P(("seq", "head"), None)
    return jax.shard_map(
        per_device, mesh=mesh, in_specs=in_specs, out_specs=out_specs, check_vma=False
    )
```

```python
import functools
import math

import jax
import jax.numpy as jnp
from jax import lax
from jax.experimental import pallas as pl
from jax.experimental.pallas import tpu as pltpu
from jax.sharding import PartitionSpec as P

BLOCK = 128
PAIRS = 16
KCAP = 4
LANES = 128
META = 16
VMEM_LIMIT = 56 * 1024 * 1024
BF16 = jnp.bfloat16
F32 = jnp.float32
I32 = jnp.int32


def dot(left, right):
    return jnp.dot(left, right, preferred_element_type=F32)


def iota(shape, dim):
    return lax.broadcasted_iota(I32, shape, dim)


def params():
    return pltpu.CompilerParams(vmem_limit_bytes=VMEM_LIMIT)


def slot_kernel(ids_ref, slot_ref, count_ref, *, groups, owned, capacity):
    clusters = groups * owned
    chunks = ids_ref.shape[1]
    row = iota((clusters, LANES), 0)
    lane = iota((clusters, LANES), 1)
    before = iota((LANES, 2 * LANES), 0)
    after = iota((LANES, 2 * LANES), 1)
    running = ((after >= LANES) | (before <= after)).astype(BF16)
    every = jnp.ones((LANES, LANES), BF16)
    counts = jnp.zeros((clusters, LANES), F32)
    for chunk in range(chunks):
        hit = (ids_ref[0, chunk : chunk + 1, :] == row).astype(BF16)
        counts = counts + dot(hit, every)
    first = iota((clusters, clusters), 0)
    second = iota((clusters, clusters), 1)
    inside = ((second < first) & (second // owned == first // owned)).astype(BF16)
    carry = dot(inside, counts.astype(BF16)) + ((row // owned) * capacity - 1).astype(F32)
    own = jnp.where(lane == row % owned, counts, 0.0).astype(BF16)
    of_group = (iota((groups, clusters), 0) == iota((groups, clusters), 1) // owned).astype(BF16)
    count_ref[0] = dot(of_group, own)
    for chunk in range(chunks):
        match = ids_ref[0, chunk : chunk + 1, :] == row
        sums = dot(match.astype(BF16), running)
        picked = jnp.where(match, sums[:, :LANES] + carry, 0.0)
        slot_ref[0, chunk : chunk + 1, :] = jnp.sum(picked, axis=0, keepdims=True).astype(I32)
        carry = carry + sums[:, LANES:]


def spread(index, rows, store, slots, step):
    flat = jnp.concatenate([index[i : i + 1, :] for i in range(index.shape[0])], axis=1)
    count = flat.shape[1]
    within = iota((step, count), 0)

    def body(i, carry):
        onehot = (flat - i * step == within).astype(BF16)
        store(i, dot(onehot, rows).astype(BF16))
        return carry

    lax.fori_loop(0, slots // step, body, 0)


def collect(index, packed, wide_ref, store, step):
    turned = index.astype(F32).T
    chunks = index.shape[0]
    for i in range(chunks):
        wide_ref[i * LANES : (i + 1) * LANES, :] = jnp.broadcast_to(
            turned[:, i : i + 1], (LANES, LANES)
        ).astype(I32)
    lane = iota((step, LANES), 1)
    tiles = packed.shape[0] // LANES

    def body(i, carry):
        wide = wide_ref[pl.ds(pl.multiple_of(i * step, step), step), :] - lane
        onehot = jnp.concatenate([(wide == t * LANES).astype(BF16) for t in range(tiles)], axis=1)
        store(i, dot(onehot, packed).astype(BF16))
        return carry

    lax.fori_loop(0, chunks * LANES // step, body, 0)


def split_kernel(key_ref, value_ref, out_ref):
    out_ref[0, 0] = key_ref[...]
    out_ref[0, 1] = value_ref[...]


def pack_kv_kernel(slot_ref, key_count_ref, query_count_ref, key_ref, value_ref, out_ref):
    groups, _, rows, _ = out_ref.shape
    capacity = rows - META
    tokens = key_ref.shape[0] * key_ref.shape[2]
    keys = key_ref[:, 0].reshape(tokens, LANES)
    values = value_ref[:, 0].reshape(tokens, LANES)

    def store(i, block):
        out_ref[pl.ds(2 * i, 2), 0, :capacity, :] = block.reshape(2, capacity, 2 * LANES)

    both = jnp.concatenate([keys, values], axis=1)
    spread(slot_ref[0], both, store, groups * capacity, 2 * capacity)
    for group in range(groups):
        key_count = jnp.broadcast_to(key_count_ref[0, group : group + 1, :], (META, LANES))
        query_count = jnp.broadcast_to(query_count_ref[0, group : group + 1, :], (META, LANES))
        out_ref[group, 0, capacity:, :LANES] = key_count.astype(BF16)
        out_ref[group, 0, capacity:, LANES:] = query_count.astype(BF16)


def pack_q_kernel(slot_ref, query_ref, out_ref):
    groups, _, capacity, _ = out_ref.shape
    tokens = query_ref.shape[0] * query_ref.shape[1]

    def store(i, block):
        out_ref[pl.ds(2 * i, 2), 0] = block.reshape(2, capacity, LANES)

    queries = query_ref[...].reshape(tokens, LANES)
    spread(slot_ref[0], queries, store, groups * capacity, 2 * capacity)


def sources(counts, capacity):
    groups = counts.shape[0]
    padded = jnp.concatenate([counts, jnp.zeros((LANES - groups, LANES), F32)], axis=0).astype(BF16)
    row = iota((LANES, LANES), 0)
    col = iota((LANES, LANES), 1)
    below = dot((col < row).astype(BF16), padded)
    offset = dot(padded, (row < col).astype(BF16))
    start = (row * capacity).astype(F32) + offset - below
    below_t = below.T[:groups]
    start_t = start.T[:groups]
    place = iota((groups, LANES), 1).astype(F32)
    found = jnp.broadcast_to(start_t[:, 0:1], (groups, LANES))
    for source in range(1, groups):
        found = jnp.where(below_t[:, source : source + 1] <= place, start_t[:, source : source + 1], found)
    return (found + place).astype(I32)


def unpack_kv_kernel(pick_ref, in_ref, out_ref, query_source_ref, wide_ref, sorted_ref, *, first):
    head = pl.program_id(0) + first
    groups, _, rows, _ = in_ref.shape
    capacity = rows - META
    counts = in_ref[:, 0, capacity:, :].astype(F32)
    counts = jnp.max(counts, axis=1)
    query_source_ref[0] = sources(counts[:, LANES:], capacity)
    packed = in_ref[:, 0, :capacity, :].reshape(groups * capacity, 2 * LANES)

    def store(i, block):
        sorted_ref[pl.ds(4 * i, 4)] = block.reshape(4, BLOCK, 2 * LANES)

    collect(sources(counts[:, :LANES], capacity), packed, wide_ref, store, 4 * BLOCK)

    def copy(i, carry):
        for j in range(KCAP):
            out_ref[i, 0, j] = sorted_ref[pick_ref[head, i, j]]
        return carry

    lax.fori_loop(0, groups, copy, 0)


def unpack_q_kernel(index_ref, in_ref, out_ref, wide_ref):
    groups, _, capacity, _ = in_ref.shape
    packed = in_ref[:, 0].reshape(groups * capacity, LANES)
    step = 4 * BLOCK

    def store(i, block):
        out_ref[0, pl.ds(pl.multiple_of(i * step, step), step), :] = block

    collect(index_ref[0], packed, wide_ref, store, step)


def final_kernel(index_ref, in_ref, *refs):
    out_ref, wide_ref = refs[-2:]
    groups, _, capacity, _ = in_ref.shape
    packed = in_ref[:, 0].reshape(groups * capacity, LANES)
    part = out_ref.shape[1]

    def store(i, block):
        out_ref[pl.ds(2 * i, 2)] = block.reshape(2, part, LANES)

    collect(index_ref[0], packed, wide_ref, store, 2 * part)


def attend_kernel(fetch_ref, index_ref, query_ref, recv_ref, out_ref, attended_ref, *, first):
    head = pl.program_id(0) + first
    groups, _, capacity, _ = out_ref.shape
    owned = query_ref.shape[1] // BLOCK
    scale = math.log2(math.e) / math.sqrt(LANES)

    def one(cluster):
        rows = pl.ds(pl.multiple_of(cluster * BLOCK, BLOCK), BLOCK)
        queries = query_ref[0, rows, :]
        blocks = []
        for pair in range(PAIRS):
            at = fetch_ref[head, cluster, pair]
            blocks.append((at // KCAP, at % KCAP))
        keys = jnp.concatenate([recv_ref[b, 0, j, :, :LANES] for b, j in blocks], axis=0)
        values = jnp.concatenate([recv_ref[b, 0, j, :, LANES:] for b, j in blocks], axis=0)
        scores = lax.dot_general(
            queries, keys, (((1,), (1,)), ((), ())), preferred_element_type=F32
        )
        weights = jnp.exp2((scores - jnp.max(scores, axis=1, keepdims=True)) * scale)
        total = jnp.sum(weights, axis=1, keepdims=True)
        mixed = dot(weights.astype(BF16), values)
        attended_ref[rows, :] = (mixed / total).astype(BF16)

    def body(i, carry):
        for j in range(4):
            one(4 * i + j)
        return carry

    lax.fori_loop(0, owned // 4, body, 0)

    def store(i, block):
        out_ref[pl.ds(2 * i, 2), 0] = block.reshape(2, capacity, LANES)

    spread(index_ref[0], attended_ref[...], store, groups * capacity, 2 * capacity)


def shape_of(shape, dtype):
    return jax.ShapeDtypeStruct(shape, dtype)


def cost(flops, moved, exps=0):
    return pl.CostEstimate(flops=int(flops), bytes_accessed=int(moved), transcendentals=int(exps))


def exchange(array, axis):
    return lax.all_to_all(array, axis, split_axis=0, concat_axis=0, tiled=True)


def tables(cluster_pairs, my_index, groups):
    heads, clusters, _ = cluster_pairs.shape
    owned = clusters // groups
    by_group = cluster_pairs.reshape(heads, groups, owned * PAIRS)
    local = jnp.arange(owned, dtype=I32)
    earlier = (local[:, None] < local[None, :]).astype(F32)
    needed = jnp.any(by_group[:, :, None, :] == (my_index * owned + local)[None, None, :, None], axis=3)
    order = jnp.einsum("hac,cd->had", needed.astype(F32), earlier).astype(I32)
    hits = needed[:, :, None, :] & (order[:, :, None, :] == jnp.arange(KCAP, dtype=I32)[:, None])
    pick = jnp.sum(jnp.where(hits, local, 0), axis=3)
    own = lax.dynamic_index_in_dim(by_group, my_index, 1, keepdims=False)
    every = jnp.arange(clusters, dtype=I32)
    same = own[:, :, None] == every
    wanted = jnp.any(same, axis=1).reshape(heads, groups, owned)
    rank = jnp.einsum("hac,cd->had", wanted.astype(F32), earlier).astype(I32)
    position = (rank + jnp.arange(groups, dtype=I32)[None, :, None] * KCAP).reshape(heads, 1, clusters)
    fetch = jnp.sum(jnp.where(same, position, 0), axis=2)
    return pick, fetch.reshape(heads, owned, PAIRS)


def per_device(query_rows, key_rows, value_rows, query_cluster, key_cluster, cluster_pairs):
    heads, tokens = query_cluster.shape
    groups = lax.axis_size("seq")
    parts = lax.axis_size("head")
    my_index = lax.axis_index("seq")
    clusters = cluster_pairs.shape[1]
    owned = clusters // groups
    capacity = 3 * tokens // (2 * groups)
    slots = groups * capacity
    part = tokens // parts
    width = heads * LANES
    chunks = tokens // LANES

    def by_part(rows):
        return rows.reshape(part, parts, width).transpose(1, 0, 2)

    kv_sent = pl.pallas_call(
        split_kernel,
        grid=(parts,),
        in_specs=[pl.BlockSpec((part, width), lambda i: (0, i))] * 2,
        out_specs=pl.BlockSpec((1, 2, part, width), lambda i: (i, 0, 0, 0)),
        out_shape=shape_of((parts, 2, part, width), BF16),
        compiler_params=params(),
        cost_estimate=cost(0, 6e6),
        name="split_kv",
    )(key_rows, value_rows)
    kv_tok = exchange(kv_sent, "head")
    q_tok = exchange(by_part(query_rows), "head")

    ids = jnp.concatenate([query_cluster, key_cluster], axis=0).reshape(2 * heads, chunks, LANES)
    slot, count = pl.pallas_call(
        functools.partial(slot_kernel, groups=groups, owned=owned, capacity=capacity),
        grid=(2 * heads,),
        in_specs=[pl.BlockSpec((1, chunks, LANES), lambda h: (h, 0, 0))],
        out_specs=[
            pl.BlockSpec((1, chunks, LANES), lambda h: (h, 0, 0)),
            pl.BlockSpec((1, groups, LANES), lambda h: (h, 0, 0)),
        ],
        out_shape=[
            shape_of((2 * heads, chunks, LANES), I32),
            shape_of((2 * heads, groups, LANES), F32),
        ],
        compiler_params=params(),
        cost_estimate=cost(2e9 * heads, 1e6),
        name="slots",
    )(ids)
    pick, fetch = tables(cluster_pairs, my_index, groups)

    kv_packed = pl.pallas_call(
        pack_kv_kernel,
        grid=(heads,),
        in_specs=[
            pl.BlockSpec((1, chunks, LANES), lambda h: (h + heads, 0, 0)),
            pl.BlockSpec((1, groups, LANES), lambda h: (h + heads, 0, 0)),
            pl.BlockSpec((1, groups, LANES), lambda h: (h, 0, 0)),
            pl.BlockSpec((parts, 1, part, LANES), lambda h: (0, 0, 0, h)),
            pl.BlockSpec((parts, 1, part, LANES), lambda h: (0, 1, 0, h)),
        ],
        out_specs=pl.BlockSpec((groups, 1, capacity + META, 2 * LANES), lambda h: (0, h, 0, 0)),
        out_shape=shape_of((groups, heads, capacity + META, 2 * LANES), BF16),
        compiler_params=params(),
        cost_estimate=cost(heads * 16.0 * slots * tokens * LANES, 8e6),
        name="pack_kv",
    )(slot, count, count, kv_tok, kv_tok)
    kv_recv = exchange(kv_packed, "seq")

    q_packed = pl.pallas_call(
        pack_q_kernel,
        grid=(heads,),
        in_specs=[
            pl.BlockSpec((1, chunks, LANES), lambda h: (h, 0, 0)),
            pl.BlockSpec((parts, part, LANES), lambda h: (0, 0, h)),
        ],
        out_specs=pl.BlockSpec((groups, 1, capacity, LANES), lambda h: (0, h, 0, 0)),
        out_shape=shape_of((groups, heads, capacity, LANES), BF16),
        compiler_params=params(),
        cost_estimate=cost(heads * 4.0 * slots * tokens * LANES, 4e6),
        name="pack_q",
    )(slot, q_tok)
    q_recv = exchange(q_packed, "seq")

    def unpack_kv(first, count_heads):
        return pl.pallas_call(
            functools.partial(unpack_kv_kernel, first=first),
            grid_spec=pltpu.PrefetchScalarGridSpec(
                num_scalar_prefetch=1,
                grid=(count_heads,),
                in_specs=[
                    pl.BlockSpec(
                        (groups, 1, capacity + META, 2 * LANES), lambda h, pick: (0, h + first, 0, 0)
                    ),
                ],
                out_specs=[
                    pl.BlockSpec(
                        (groups, 1, KCAP, BLOCK, 2 * LANES), lambda h, pick: (0, h, 0, 0, 0)
                    ),
                    pl.BlockSpec((1, owned, BLOCK), lambda h, pick: (h, 0, 0)),
                ],
                scratch_shapes=[
                    pltpu.VMEM((owned * BLOCK, LANES), I32),
                    pltpu.VMEM((owned, BLOCK, 2 * LANES), BF16),
                ],
            ),
            out_shape=[
                shape_of((groups, count_heads, KCAP, BLOCK, 2 * LANES), BF16),
                shape_of((count_heads, owned, BLOCK), I32),
            ],
            compiler_params=params(),
            cost_estimate=cost(count_heads * 4.0 * slots * tokens * LANES, count_heads * 6e6),
            name=f"unpack_kv_{first}",
        )(pick, kv_recv)

    splits = ((0, heads - 1), (heads - 1, 1))
    received = []
    indices = []
    for first, count_heads in splits:
        sent, index = unpack_kv(first, count_heads)
        indices.append(index)
        received.append(exchange(sent, "seq"))
    index = jnp.concatenate(indices, axis=0)

    q_sorted = pl.pallas_call(
        unpack_q_kernel,
        grid=(heads,),
        in_specs=[
            pl.BlockSpec((1, owned, BLOCK), lambda h: (h, 0, 0)),
            pl.BlockSpec((groups, 1, capacity, LANES), lambda h: (0, h, 0, 0)),
        ],
        out_specs=pl.BlockSpec((1, owned * BLOCK, LANES), lambda h: (h, 0, 0)),
        out_shape=shape_of((heads, owned * BLOCK, LANES), BF16),
        scratch_shapes=[pltpu.VMEM((owned * BLOCK, LANES), I32)],
        compiler_params=params(),
        cost_estimate=cost(heads * 4.0 * slots * tokens * LANES, 4e6),
        name="unpack_q",
    )(index, q_recv)

    token_rows = None
    for (first, count_heads), recv in zip(splits, received, strict=True):
        reply = pl.pallas_call(
            functools.partial(attend_kernel, first=first),
            grid_spec=pltpu.PrefetchScalarGridSpec(
                num_scalar_prefetch=1,
                grid=(count_heads,),
                in_specs=[
                    pl.BlockSpec((1, owned, BLOCK), lambda h, fetch, first=first: (h + first, 0, 0)),
                    pl.BlockSpec(
                        (1, owned * BLOCK, LANES), lambda h, fetch, first=first: (h + first, 0, 0)
                    ),
                    pl.BlockSpec(
                        (groups, 1, KCAP, BLOCK, 2 * LANES), lambda h, fetch: (0, h, 0, 0, 0)
                    ),
                ],
                out_specs=pl.BlockSpec((groups, 1, capacity, LANES), lambda h, fetch: (0, h, 0, 0)),
                scratch_shapes=[pltpu.VMEM((owned * BLOCK, LANES), BF16)],
            ),
            out_shape=shape_of((groups, count_heads, capacity, LANES), BF16),
            compiler_params=params(),
            cost_estimate=cost(
                count_heads * 4.0 * owned * BLOCK * PAIRS * BLOCK * LANES,
                count_heads * 6e6,
                count_heads * owned * BLOCK * PAIRS * BLOCK,
            ),
            name=f"attend_{first}",
        )(fetch, index, q_sorted, recv)
        returned = exchange(reply, "seq")
        operands = (slot, returned) + (() if token_rows is None else (token_rows,))
        token_rows = pl.pallas_call(
            final_kernel,
            grid=(count_heads,),
            in_specs=[
                pl.BlockSpec((1, chunks, LANES), lambda h, first=first: (h + first, 0, 0)),
                pl.BlockSpec((groups, 1, capacity, LANES), lambda h: (0, h, 0, 0)),
            ]
            + [pl.BlockSpec(memory_space=pl.ANY)] * (len(operands) - 2),
            out_specs=pl.BlockSpec((parts, part, LANES), lambda h, first=first: (0, 0, h + first)),
            out_shape=shape_of((parts, part, width), BF16),
            scratch_shapes=[pltpu.VMEM((tokens, LANES), I32)],
            input_output_aliases={} if token_rows is None else {2: 0},
            compiler_params=params(),
            cost_estimate=cost(count_heads * 4.0 * slots * tokens * LANES, 2e6),
            name=f"final_{first}",
        )(*operands)
    rows = exchange(token_rows, "head")
    return rows.transpose(1, 0, 2).reshape(part, parts * width)


def solution(mesh):
    in_specs = (
        P(("seq", "head"), None),
        P(("seq", "head"), None),
        P(("seq", "head"), None),
        P("head", "seq"),
        P("head", "seq"),
        P("head", None, None),
    )
    out_specs = P(("seq", "head"), None)
    return jax.shard_map(
        per_device, mesh=mesh, in_specs=in_specs, out_specs=out_specs, check_vma=False
    )
```

```python
import functools
import math

import jax
import jax.numpy as jnp
from jax import lax
from jax.experimental import pallas as pl
from jax.experimental.pallas import tpu as pltpu
from jax.sharding import PartitionSpec as P

BLOCK = 128
PAIRS = 16
KCAP = 4
LANES = 128
META = 16
VMEM_LIMIT = 56 * 1024 * 1024
BF16 = jnp.bfloat16
F32 = jnp.float32
I32 = jnp.int32


def dot(left, right):
    return jnp.dot(left, right, preferred_element_type=F32)


def iota(shape, dim):
    return lax.broadcasted_iota(I32, shape, dim)


def params():
    return pltpu.CompilerParams(vmem_limit_bytes=VMEM_LIMIT)


def slot_kernel(ids_ref, slot_ref, count_ref, *, groups, owned, capacity):
    clusters = groups * owned
    chunks = ids_ref.shape[1]
    row = iota((clusters, LANES), 0)
    lane = iota((clusters, LANES), 1)
    before = iota((LANES, 2 * LANES), 0)
    after = iota((LANES, 2 * LANES), 1)
    running = ((after >= LANES) | (before <= after)).astype(BF16)
    every = jnp.ones((LANES, LANES), BF16)
    counts = jnp.zeros((clusters, LANES), F32)
    for chunk in range(chunks):
        hit = (ids_ref[0, chunk : chunk + 1, :] == row).astype(BF16)
        counts = counts + dot(hit, every)
    first = iota((clusters, clusters), 0)
    second = iota((clusters, clusters), 1)
    inside = ((second < first) & (second // owned == first // owned)).astype(BF16)
    carry = dot(inside, counts.astype(BF16)) + ((row // owned) * capacity - 1).astype(F32)
    own = jnp.where(lane == row % owned, counts, 0.0).astype(BF16)
    of_group = (iota((groups, clusters), 0) == iota((groups, clusters), 1) // owned).astype(BF16)
    count_ref[0] = dot(of_group, own)
    for chunk in range(chunks):
        match = ids_ref[0, chunk : chunk + 1, :] == row
        sums = dot(match.astype(BF16), running)
        picked = jnp.where(match, sums[:, :LANES] + carry, 0.0)
        slot_ref[0, chunk : chunk + 1, :] = jnp.sum(picked, axis=0, keepdims=True).astype(I32)
        carry = carry + sums[:, LANES:]


def spread(index, rows, store, slots, step):
    flat = jnp.concatenate([index[i : i + 1, :] for i in range(index.shape[0])], axis=1)
    count = flat.shape[1]
    within = iota((step, count), 0)

    def body(i, carry):
        onehot = (flat - i * step == within).astype(BF16)
        store(i, dot(onehot, rows).astype(BF16))
        return carry

    lax.fori_loop(0, slots // step, body, 0)


def collect(index, packed, wide_ref, store, step):
    turned = index.astype(F32).T
    chunks = index.shape[0]
    for i in range(chunks):
        wide_ref[i * LANES : (i + 1) * LANES, :] = jnp.broadcast_to(
            turned[:, i : i + 1], (LANES, LANES)
        ).astype(I32)
    lane = iota((step, LANES), 1)
    tiles = packed.shape[0] // LANES

    def body(i, carry):
        wide = wide_ref[pl.ds(pl.multiple_of(i * step, step), step), :] - lane
        onehot = jnp.concatenate([(wide == t * LANES).astype(BF16) for t in range(tiles)], axis=1)
        store(i, dot(onehot, packed).astype(BF16))
        return carry

    lax.fori_loop(0, chunks * LANES // step, body, 0)


def split_kernel(key_ref, value_ref, out_ref):
    parts, _, _, width = out_ref.shape
    for part in range(parts):
        columns = slice(part * width, (part + 1) * width)
        out_ref[part, 0] = key_ref[:, columns]
        out_ref[part, 1] = value_ref[:, columns]


def pack_kv_kernel(slot_ref, count_ref, key_ref, value_ref, out_ref):
    head = pl.program_id(0)
    heads = pl.num_programs(0)
    groups, rows, _ = out_ref.shape
    of_heads = count_ref.shape[0] // 2
    capacity = (rows - META) // of_heads
    tokens = key_ref.shape[0] * key_ref.shape[2]
    keys = key_ref[:, 0].reshape(tokens, LANES)
    values = value_ref[:, 0].reshape(tokens, LANES)
    at = pl.ds(pl.multiple_of(head * capacity, META), capacity)

    def store(i, block):
        out_ref[pl.ds(2 * i, 2), at, :] = block.reshape(2, capacity, 2 * LANES)

    both = jnp.concatenate([keys, values], axis=1)
    spread(slot_ref[0], both, store, groups * capacity, 2 * capacity)

    @pl.when(head == heads - 1)
    def _():
        row = iota((groups, META, LANES), 1)
        for side in range(2):
            block = jnp.zeros((groups, META, LANES), F32)
            for h in range(of_heads):
                counts = count_ref[(1 - side) * of_heads + h]
                block = jnp.where(row == h, counts[:, None, :], block)
            out_ref[:, of_heads * capacity :, side * LANES : (side + 1) * LANES] = block.astype(BF16)


def pack_q_kernel(slot_ref, query_ref, out_ref):
    groups, _, capacity, _ = out_ref.shape
    tokens = query_ref.shape[0] * query_ref.shape[1]

    def store(i, block):
        out_ref[pl.ds(2 * i, 2), 0] = block.reshape(2, capacity, LANES)

    queries = query_ref[...].reshape(tokens, LANES)
    spread(slot_ref[0], queries, store, groups * capacity, 2 * capacity)


def sources(counts, capacity):
    groups = counts.shape[0]
    padded = jnp.concatenate([counts, jnp.zeros((LANES - groups, LANES), F32)], axis=0).astype(BF16)
    row = iota((LANES, LANES), 0)
    col = iota((LANES, LANES), 1)
    below = dot((col < row).astype(BF16), padded)
    offset = dot(padded, (row < col).astype(BF16))
    start = (row * capacity).astype(F32) + offset - below
    below_t = below.T[:groups]
    start_t = start.T[:groups]
    place = iota((groups, LANES), 1).astype(F32)
    found = jnp.broadcast_to(start_t[:, 0:1], (groups, LANES))
    for source in range(1, groups):
        found = jnp.where(below_t[:, source : source + 1] <= place, start_t[:, source : source + 1], found)
    return (found + place).astype(I32)


def unpack_kv_kernel(
    pick_ref, in_ref, meta_ref, first_ref, last_ref, query_source_ref, wide_ref, sorted_ref
):
    head = pl.program_id(0)
    heads = pl.num_programs(0)
    groups, capacity, _ = in_ref.shape
    row = iota(meta_ref.shape, 1)
    counts = jnp.sum(jnp.where(row == head, meta_ref[...].astype(F32), 0.0), axis=1)
    query_source_ref[0] = sources(counts[:, LANES:], capacity)
    packed = in_ref[...].reshape(groups * capacity, 2 * LANES)

    def store(i, block):
        sorted_ref[pl.ds(4 * i, 4)] = block.reshape(4, BLOCK, 2 * LANES)

    collect(sources(counts[:, :LANES], capacity), packed, wide_ref, store, 4 * BLOCK)

    def send(out_ref):
        def copy(i, carry):
            for j in range(KCAP):
                out_ref[i, 0, j] = sorted_ref[pick_ref[head, i, j]]
            return carry

        lax.fori_loop(0, groups, copy, 0)

    @pl.when(head < heads - 1)
    def _():
        send(first_ref)

    @pl.when(head == heads - 1)
    def _():
        send(last_ref)


def unpack_q_kernel(index_ref, in_ref, out_ref, wide_ref):
    groups, _, capacity, _ = in_ref.shape
    packed = in_ref[:, 0].reshape(groups * capacity, LANES)
    step = 4 * BLOCK

    def store(i, block):
        out_ref[0, pl.ds(pl.multiple_of(i * step, step), step), :] = block

    collect(index_ref[0], packed, wide_ref, store, step)


def final_kernel(index_ref, in_ref, *refs):
    out_ref, wide_ref = refs[-2:]
    groups, _, capacity, _ = in_ref.shape
    packed = in_ref[:, 0].reshape(groups * capacity, LANES)
    part = out_ref.shape[1]

    def store(i, block):
        out_ref[pl.ds(2 * i, 2)] = block.reshape(2, part, LANES)

    collect(index_ref[0], packed, wide_ref, store, 2 * part)


def attend_kernel(fetch_ref, index_ref, query_ref, recv_ref, out_ref, attended_ref, *, first):
    head = pl.program_id(0) + first
    groups, _, capacity, _ = out_ref.shape
    owned = query_ref.shape[1] // BLOCK
    scale = math.log2(math.e) / math.sqrt(LANES)

    def one(cluster):
        rows = pl.ds(pl.multiple_of(cluster * BLOCK, BLOCK), BLOCK)
        queries = query_ref[0, rows, :]
        blocks = []
        for pair in range(PAIRS):
            at = fetch_ref[head, cluster, pair]
            blocks.append((at // KCAP, at % KCAP))
        keys = jnp.concatenate([recv_ref[b, 0, j, :, :LANES] for b, j in blocks], axis=0)
        values = jnp.concatenate([recv_ref[b, 0, j, :, LANES:] for b, j in blocks], axis=0)
        scores = lax.dot_general(
            queries, keys, (((1,), (1,)), ((), ())), preferred_element_type=F32
        )
        weights = jnp.exp2((scores - jnp.max(scores, axis=1, keepdims=True)) * scale)
        total = jnp.sum(weights, axis=1, keepdims=True)
        mixed = dot(weights.astype(BF16), values)
        attended_ref[rows, :] = (mixed / total).astype(BF16)

    def body(i, carry):
        for j in range(4):
            one(4 * i + j)
        return carry

    lax.fori_loop(0, owned // 4, body, 0)

    def store(i, block):
        out_ref[pl.ds(2 * i, 2), 0] = block.reshape(2, capacity, LANES)

    spread(index_ref[0], attended_ref[...], store, groups * capacity, 2 * capacity)


def shape_of(shape, dtype):
    return jax.ShapeDtypeStruct(shape, dtype)


def cost(flops, moved, exps=0):
    return pl.CostEstimate(flops=int(flops), bytes_accessed=int(moved), transcendentals=int(exps))


def exchange(array, axis):
    return lax.all_to_all(array, axis, split_axis=0, concat_axis=0, tiled=True)


def tables(cluster_pairs, my_index, groups):
    heads, clusters, _ = cluster_pairs.shape
    owned = clusters // groups
    by_group = cluster_pairs.reshape(heads, groups, owned * PAIRS)
    local = jnp.arange(owned, dtype=I32)
    earlier = (local[:, None] < local[None, :]).astype(F32)
    needed = jnp.any(by_group[:, :, None, :] == (my_index * owned + local)[None, None, :, None], axis=3)
    order = jnp.einsum("hac,cd->had", needed.astype(F32), earlier).astype(I32)
    hits = needed[:, :, None, :] & (order[:, :, None, :] == jnp.arange(KCAP, dtype=I32)[:, None])
    pick = jnp.sum(jnp.where(hits, local, 0), axis=3)
    own = lax.dynamic_index_in_dim(by_group, my_index, 1, keepdims=False)
    every = jnp.arange(clusters, dtype=I32)
    same = own[:, :, None] == every
    wanted = jnp.any(same, axis=1).reshape(heads, groups, owned)
    rank = jnp.einsum("hac,cd->had", wanted.astype(F32), earlier).astype(I32)
    position = (rank + jnp.arange(groups, dtype=I32)[None, :, None] * KCAP).reshape(heads, 1, clusters)
    fetch = jnp.sum(jnp.where(same, position, 0), axis=2)
    return pick, fetch.reshape(heads, owned, PAIRS)


def per_device(query_rows, key_rows, value_rows, query_cluster, key_cluster, cluster_pairs):
    heads, tokens = query_cluster.shape
    groups = lax.axis_size("seq")
    parts = lax.axis_size("head")
    my_index = lax.axis_index("seq")
    clusters = cluster_pairs.shape[1]
    owned = clusters // groups
    capacity = 3 * tokens // (2 * groups)
    slots = groups * capacity
    part = tokens // parts
    width = heads * LANES
    chunks = tokens // LANES

    def by_part(rows):
        return rows.reshape(part, parts, width).transpose(1, 0, 2)

    kv_sent = pl.pallas_call(
        split_kernel,
        grid=(4,),
        in_specs=[pl.BlockSpec((part // 4, parts * width), lambda i: (i, 0))] * 2,
        out_specs=pl.BlockSpec((parts, 2, part // 4, width), lambda i: (0, 0, i, 0)),
        out_shape=shape_of((parts, 2, part, width), BF16),
        compiler_params=params(),
        cost_estimate=cost(0, 6e6),
        name="split_kv",
    )(key_rows, value_rows)
    kv_tok = exchange(kv_sent, "head")
    q_tok = exchange(by_part(query_rows), "head")

    ids = jnp.concatenate([query_cluster, key_cluster], axis=0).reshape(2 * heads, chunks, LANES)
    slot, count = pl.pallas_call(
        functools.partial(slot_kernel, groups=groups, owned=owned, capacity=capacity),
        grid=(2 * heads,),
        in_specs=[pl.BlockSpec((1, chunks, LANES), lambda h: (h, 0, 0))],
        out_specs=[
            pl.BlockSpec((1, chunks, LANES), lambda h: (h, 0, 0)),
            pl.BlockSpec((1, groups, LANES), lambda h: (h, 0, 0)),
        ],
        out_shape=[
            shape_of((2 * heads, chunks, LANES), I32),
            shape_of((2 * heads, groups, LANES), F32),
        ],
        compiler_params=params(),
        cost_estimate=cost(2e9 * heads, 1e6),
        name="slots",
    )(ids)
    pick, fetch = tables(cluster_pairs, my_index, groups)

    kv_packed = pl.pallas_call(
        pack_kv_kernel,
        grid=(heads,),
        in_specs=[
            pl.BlockSpec((1, chunks, LANES), lambda h: (h + heads, 0, 0)),
            pl.BlockSpec((2 * heads, groups, LANES), lambda h: (0, 0, 0)),
            pl.BlockSpec((parts, 1, part, LANES), lambda h: (0, 0, 0, h)),
            pl.BlockSpec((parts, 1, part, LANES), lambda h: (0, 1, 0, h)),
        ],
        out_specs=pl.BlockSpec((groups, heads * capacity + META, 2 * LANES), lambda h: (0, 0, 0)),
        out_shape=shape_of((groups, heads * capacity + META, 2 * LANES), BF16),
        compiler_params=params(),
        cost_estimate=cost(heads * 16.0 * slots * tokens * LANES, 8e6),
        name="pack_kv",
    )(slot, count, kv_tok, kv_tok)
    kv_recv = exchange(kv_packed, "seq")

    q_packed = pl.pallas_call(
        pack_q_kernel,
        grid=(heads,),
        in_specs=[
            pl.BlockSpec((1, chunks, LANES), lambda h: (h, 0, 0)),
            pl.BlockSpec((parts, part, LANES), lambda h: (0, 0, h)),
        ],
        out_specs=pl.BlockSpec((groups, 1, capacity, LANES), lambda h: (0, h, 0, 0)),
        out_shape=shape_of((groups, heads, capacity, LANES), BF16),
        compiler_params=params(),
        cost_estimate=cost(heads * 4.0 * slots * tokens * LANES, 4e6),
        name="pack_q",
    )(slot, q_tok)
    q_recv = exchange(q_packed, "seq")

    splits = ((0, heads - 1), (heads - 1, 1))
    block = (groups, 1, KCAP, BLOCK, 2 * LANES)
    first_sent, last_sent, index = pl.pallas_call(
        unpack_kv_kernel,
        grid_spec=pltpu.PrefetchScalarGridSpec(
            num_scalar_prefetch=1,
            grid=(heads,),
            in_specs=[
                pl.BlockSpec((groups, capacity, 2 * LANES), lambda h, pick: (0, h, 0)),
                pl.BlockSpec(
                    (groups, META, 2 * LANES), lambda h, pick: (0, heads * capacity // META, 0)
                ),
            ],
            out_specs=[
                pl.BlockSpec(block, lambda h, pick: (0, jnp.minimum(h, heads - 2), 0, 0, 0)),
                pl.BlockSpec(block, lambda h, pick: (0, 0, 0, 0, 0)),
                pl.BlockSpec((1, owned, BLOCK), lambda h, pick: (h, 0, 0)),
            ],
            scratch_shapes=[
                pltpu.VMEM((owned * BLOCK, LANES), I32),
                pltpu.VMEM((owned, BLOCK, 2 * LANES), BF16),
            ],
        ),
        out_shape=[
            shape_of((groups, heads - 1, KCAP, BLOCK, 2 * LANES), BF16),
            shape_of(block, BF16),
            shape_of((heads, owned, BLOCK), I32),
        ],
        compiler_params=params(),
        cost_estimate=cost(heads * 4.0 * slots * tokens * LANES, heads * 6e6),
        name="unpack_kv",
    )(pick, kv_recv, kv_recv)
    first_recv = exchange(first_sent, "seq")
    last_recv = exchange(last_sent, "seq")
    received = (first_recv, last_recv)
    q_recv, index, _ = lax.optimization_barrier((q_recv, index, first_recv))

    q_sorted = pl.pallas_call(
        unpack_q_kernel,
        grid=(heads,),
        in_specs=[
            pl.BlockSpec((1, owned, BLOCK), lambda h: (h, 0, 0)),
            pl.BlockSpec((groups, 1, capacity, LANES), lambda h: (0, h, 0, 0)),
        ],
        out_specs=pl.BlockSpec((1, owned * BLOCK, LANES), lambda h: (h, 0, 0)),
        out_shape=shape_of((heads, owned * BLOCK, LANES), BF16),
        scratch_shapes=[pltpu.VMEM((owned * BLOCK, LANES), I32)],
        compiler_params=params(),
        cost_estimate=cost(heads * 4.0 * slots * tokens * LANES, 4e6),
        name="unpack_q",
    )(index, q_recv)

    token_rows = None
    for (first, count_heads), recv in zip(splits, received, strict=True):
        reply = pl.pallas_call(
            functools.partial(attend_kernel, first=first),
            grid_spec=pltpu.PrefetchScalarGridSpec(
                num_scalar_prefetch=1,
                grid=(count_heads,),
                in_specs=[
                    pl.BlockSpec((1, owned, BLOCK), lambda h, fetch, first=first: (h + first, 0, 0)),
                    pl.BlockSpec(
                        (1, owned * BLOCK, LANES), lambda h, fetch, first=first: (h + first, 0, 0)
                    ),
                    pl.BlockSpec(
                        (groups, 1, KCAP, BLOCK, 2 * LANES), lambda h, fetch: (0, h, 0, 0, 0)
                    ),
                ],
                out_specs=pl.BlockSpec((groups, 1, capacity, LANES), lambda h, fetch: (0, h, 0, 0)),
                scratch_shapes=[pltpu.VMEM((owned * BLOCK, LANES), BF16)],
            ),
            out_shape=shape_of((groups, count_heads, capacity, LANES), BF16),
            compiler_params=params(),
            cost_estimate=cost(
                count_heads * 4.0 * owned * BLOCK * PAIRS * BLOCK * LANES,
                count_heads * 6e6,
                count_heads * owned * BLOCK * PAIRS * BLOCK,
            ),
            name=f"attend_{first}",
        )(fetch, index, q_sorted, recv)
        returned = exchange(reply, "seq")
        operands = (slot, returned) + (() if token_rows is None else (token_rows,))
        token_rows = pl.pallas_call(
            final_kernel,
            grid=(count_heads,),
            in_specs=[
                pl.BlockSpec((1, chunks, LANES), lambda h, first=first: (h + first, 0, 0)),
                pl.BlockSpec((groups, 1, capacity, LANES), lambda h: (0, h, 0, 0)),
            ]
            + [pl.BlockSpec(memory_space=pl.ANY)] * (len(operands) - 2),
            out_specs=pl.BlockSpec((parts, part, LANES), lambda h, first=first: (0, 0, h + first)),
            out_shape=shape_of((parts, part, width), BF16),
            scratch_shapes=[pltpu.VMEM((tokens, LANES), I32)],
            input_output_aliases={} if token_rows is None else {2: 0},
            compiler_params=params(),
            cost_estimate=cost(count_heads * 4.0 * slots * tokens * LANES, 2e6),
            name=f"final_{first}",
        )(*operands)
    rows = exchange(token_rows, "head")
    return rows.transpose(1, 0, 2).reshape(part, parts * width)


def solution(mesh):
    in_specs = (
        P(("seq", "head"), None),
        P(("seq", "head"), None),
        P(("seq", "head"), None),
        P("head", "seq"),
        P("head", "seq"),
        P("head", None, None),
    )
    out_specs = P(("seq", "head"), None)
    return jax.shard_map(
        per_device, mesh=mesh, in_specs=in_specs, out_specs=out_specs, check_vma=False
    )
```

```python
import functools
import math

import jax
import jax.numpy as jnp
from jax import lax
from jax.experimental import pallas as pl
from jax.experimental.pallas import tpu as pltpu
from jax.sharding import PartitionSpec as P

BLOCK = 128
PAIRS = 16
KCAP = 4
LANES = 128
META = 16
VMEM_LIMIT = 56 * 1024 * 1024
BF16 = jnp.bfloat16
F32 = jnp.float32
I32 = jnp.int32


def dot(left, right):
    return jnp.dot(left, right, preferred_element_type=F32)


def iota(shape, dim):
    return lax.broadcasted_iota(I32, shape, dim)


def params():
    return pltpu.CompilerParams(vmem_limit_bytes=VMEM_LIMIT)


def slot_kernel(ids_ref, slot_ref, count_ref, *, groups, owned, capacity):
    clusters = groups * owned
    chunks = ids_ref.shape[1]
    row = iota((clusters, LANES), 0)
    lane = iota((clusters, LANES), 1)
    before = iota((LANES, 2 * LANES), 0)
    after = iota((LANES, 2 * LANES), 1)
    running = ((after >= LANES) | (before <= after)).astype(BF16)
    every = jnp.ones((LANES, LANES), BF16)
    counts = jnp.zeros((clusters, LANES), F32)
    for chunk in range(chunks):
        hit = (ids_ref[0, chunk : chunk + 1, :] == row).astype(BF16)
        counts = counts + dot(hit, every)
    first = iota((clusters, clusters), 0)
    second = iota((clusters, clusters), 1)
    inside = ((second < first) & (second // owned == first // owned)).astype(BF16)
    carry = dot(inside, counts.astype(BF16)) + ((row // owned) * capacity - 1).astype(F32)
    own = jnp.where(lane == row % owned, counts, 0.0).astype(BF16)
    of_group = (iota((groups, clusters), 0) == iota((groups, clusters), 1) // owned).astype(BF16)
    count_ref[0] = dot(of_group, own)
    for chunk in range(chunks):
        match = ids_ref[0, chunk : chunk + 1, :] == row
        sums = dot(match.astype(BF16), running)
        picked = jnp.where(match, sums[:, :LANES] + carry, 0.0)
        slot_ref[0, chunk : chunk + 1, :] = jnp.sum(picked, axis=0, keepdims=True).astype(I32)
        carry = carry + sums[:, LANES:]


def spread(index, rows, store, slots, step):
    flat = jnp.concatenate([index[i : i + 1, :] for i in range(index.shape[0])], axis=1)
    count = flat.shape[1]
    within = iota((step, count), 0)

    def body(i, carry):
        onehot = (flat - i * step == within).astype(BF16)
        store(i, dot(onehot, rows).astype(BF16))
        return carry

    lax.fori_loop(0, slots // step, body, 0)


def collect(index, packed, wide_ref, store, step):
    turned = index.astype(F32).T
    chunks = index.shape[0]
    for i in range(chunks):
        wide_ref[i * LANES : (i + 1) * LANES, :] = jnp.broadcast_to(
            turned[:, i : i + 1], (LANES, LANES)
        ).astype(I32)
    lane = iota((step, LANES), 1)
    tiles = packed.shape[0] // LANES

    def body(i, carry):
        wide = wide_ref[pl.ds(pl.multiple_of(i * step, step), step), :] - lane
        onehot = jnp.concatenate([(wide == t * LANES).astype(BF16) for t in range(tiles)], axis=1)
        store(i, dot(onehot, packed).astype(BF16))
        return carry

    lax.fori_loop(0, chunks * LANES // step, body, 0)


def split_kernel(key_ref, value_ref, out_ref):
    parts, _, _, width = out_ref.shape
    stride = key_ref.shape[1] // parts
    for part in range(parts):
        columns = slice(part * stride, part * stride + width)
        out_ref[part, 0] = key_ref[:, columns]
        out_ref[part, 1] = value_ref[:, columns]


def split_rest_kernel(me_ref, key_ref, value_ref, query_ref, *out_refs):
    parts = len(out_refs) // 2
    stride = key_ref.shape[1] // parts
    me = me_ref[0]
    for k in range(parts):
        start = jnp.bitwise_xor(me, k) * stride
        last = pl.ds(pl.multiple_of(start + stride - LANES, LANES), LANES)
        out_refs[k][0] = key_ref[:, last]
        out_refs[k][1] = value_ref[:, last]
        out_refs[parts + k][...] = query_ref[:, pl.ds(pl.multiple_of(start, LANES), stride)]


def partner_order(me, index, parts):
    each = index.shape[0] // parts
    row = iota(index.shape, 0)
    rows = []
    for k in range(parts):
        for j in range(each):
            wanted = jnp.bitwise_xor(me, k) * each + j
            rows.append(jnp.sum(jnp.where(row == wanted, index, 0), axis=0, keepdims=True))
    return jnp.concatenate(rows, axis=0)


def pack_kv_kernel(slot_ref, count_ref, key_ref, value_ref, out_ref):
    head = pl.program_id(0)
    heads = pl.num_programs(0)
    groups, rows, _ = out_ref.shape
    of_heads = count_ref.shape[0] // 2
    capacity = (rows - META) // (of_heads - 1)
    tokens = key_ref.shape[0] * key_ref.shape[2]
    keys = key_ref[:, 0].reshape(tokens, LANES)
    values = value_ref[:, 0].reshape(tokens, LANES)
    at = pl.ds(pl.multiple_of(head * capacity, META), capacity)

    def store(i, block):
        out_ref[pl.ds(2 * i, 2), at, :] = block.reshape(2, capacity, 2 * LANES)

    both = jnp.concatenate([keys, values], axis=1)
    spread(slot_ref[0], both, store, groups * capacity, 2 * capacity)

    @pl.when(head == heads - 1)
    def _():
        row = iota((groups, META, LANES), 1)
        for side in range(2):
            block = jnp.zeros((groups, META, LANES), F32)
            for h in range(of_heads):
                counts = count_ref[(1 - side) * of_heads + h]
                block = jnp.where(row == h, counts[:, None, :], block)
            out_ref[:, rows - META :, side * LANES : (side + 1) * LANES] = block.astype(BF16)


def pack_last_kernel(me_ref, slot_ref, *refs):
    *part_refs, out_ref = refs
    groups, capacity, _ = out_ref.shape
    index = partner_order(me_ref[0], slot_ref[0], len(part_refs))
    keys = jnp.concatenate([ref[0] for ref in part_refs], axis=0)
    values = jnp.concatenate([ref[1] for ref in part_refs], axis=0)

    def store(i, block):
        out_ref[pl.ds(2 * i, 2)] = block.reshape(2, capacity, 2 * LANES)

    both = jnp.concatenate([keys, values], axis=1)
    spread(index, both, store, groups * capacity, 2 * capacity)


def pack_q_kernel(me_ref, slot_ref, *refs):
    *part_refs, out_ref = refs
    groups, _, capacity, _ = out_ref.shape
    index = partner_order(me_ref[0], slot_ref[0], len(part_refs))
    queries = jnp.concatenate([ref[...] for ref in part_refs], axis=0)

    def store(i, block):
        out_ref[pl.ds(2 * i, 2), 0] = block.reshape(2, capacity, LANES)

    spread(index, queries, store, groups * capacity, 2 * capacity)


def sources(counts, capacity):
    groups = counts.shape[0]
    padded = jnp.concatenate([counts, jnp.zeros((LANES - groups, LANES), F32)], axis=0).astype(BF16)
    row = iota((LANES, LANES), 0)
    col = iota((LANES, LANES), 1)
    below = dot((col < row).astype(BF16), padded)
    offset = dot(padded, (row < col).astype(BF16))
    start = (row * capacity).astype(F32) + offset - below
    below_t = below.T[:groups]
    start_t = start.T[:groups]
    place = iota((groups, LANES), 1).astype(F32)
    found = jnp.broadcast_to(start_t[:, 0:1], (groups, LANES))
    for source in range(1, groups):
        found = jnp.where(below_t[:, source : source + 1] <= place, start_t[:, source : source + 1], found)
    return (found + place).astype(I32)


def unpack_kv_kernel(
    pick_ref,
    in_ref,
    last_in_ref,
    meta_ref,
    first_ref,
    last_ref,
    query_source_ref,
    wide_ref,
    sorted_ref,
):
    head = pl.program_id(0)
    heads = pl.num_programs(0)
    groups, capacity, _ = in_ref.shape
    row = iota(meta_ref.shape, 1)
    counts = jnp.sum(jnp.where(row == head, meta_ref[...].astype(F32), 0.0), axis=1)
    query_source_ref[0] = sources(counts[:, LANES:], capacity)
    key_source = sources(counts[:, :LANES], capacity)

    def store(i, block):
        sorted_ref[pl.ds(4 * i, 4)] = block.reshape(4, BLOCK, 2 * LANES)

    def send(packed_ref, out_ref):
        packed = packed_ref[...].reshape(groups * capacity, 2 * LANES)
        collect(key_source, packed, wide_ref, store, 4 * BLOCK)

        def copy(i, carry):
            for j in range(KCAP):
                out_ref[i, 0, j] = sorted_ref[pick_ref[head, i, j]]
            return carry

        lax.fori_loop(0, groups, copy, 0)

    @pl.when(head < heads - 1)
    def _():
        send(in_ref, first_ref)

    @pl.when(head == heads - 1)
    def _():
        send(last_in_ref, last_ref)


def unpack_q_kernel(index_ref, in_ref, out_ref, wide_ref):
    groups, _, capacity, _ = in_ref.shape
    packed = in_ref[:, 0].reshape(groups * capacity, LANES)
    step = 4 * BLOCK

    def store(i, block):
        out_ref[0, pl.ds(pl.multiple_of(i * step, step), step), :] = block

    collect(index_ref[0], packed, wide_ref, store, step)


def final_kernel(index_ref, in_ref, *refs):
    out_ref, wide_ref = refs[-2:]
    groups, _, capacity, _ = in_ref.shape
    packed = in_ref[:, 0].reshape(groups * capacity, LANES)
    part = out_ref.shape[1]

    def store(i, block):
        out_ref[pl.ds(2 * i, 2)] = block.reshape(2, part, LANES)

    collect(index_ref[0], packed, wide_ref, store, 2 * part)


def attend_kernel(fetch_ref, index_ref, query_ref, recv_ref, out_ref, attended_ref, *, first):
    head = pl.program_id(0) + first
    groups, _, capacity, _ = out_ref.shape
    owned = query_ref.shape[1] // BLOCK
    scale = math.log2(math.e) / math.sqrt(LANES)

    def one(cluster):
        rows = pl.ds(pl.multiple_of(cluster * BLOCK, BLOCK), BLOCK)
        queries = query_ref[0, rows, :]
        blocks = []
        for pair in range(PAIRS):
            at = fetch_ref[head, cluster, pair]
            blocks.append((at // KCAP, at % KCAP))
        keys = jnp.concatenate([recv_ref[b, 0, j, :, :LANES] for b, j in blocks], axis=0)
        values = jnp.concatenate([recv_ref[b, 0, j, :, LANES:] for b, j in blocks], axis=0)
        scores = lax.dot_general(
            queries, keys, (((1,), (1,)), ((), ())), preferred_element_type=F32
        )
        weights = jnp.exp2((scores - jnp.max(scores, axis=1, keepdims=True)) * scale)
        total = jnp.sum(weights, axis=1, keepdims=True)
        mixed = dot(weights.astype(BF16), values)
        attended_ref[rows, :] = (mixed / total).astype(BF16)

    def body(i, carry):
        for j in range(4):
            one(4 * i + j)
        return carry

    lax.fori_loop(0, owned // 4, body, 0)

    def store(i, block):
        out_ref[pl.ds(2 * i, 2), 0] = block.reshape(2, capacity, LANES)

    spread(index_ref[0], attended_ref[...], store, groups * capacity, 2 * capacity)


def shape_of(shape, dtype):
    return jax.ShapeDtypeStruct(shape, dtype)


def cost(flops, moved, exps=0):
    return pl.CostEstimate(flops=int(flops), bytes_accessed=int(moved), transcendentals=int(exps))


def exchange(array, axis):
    return lax.all_to_all(array, axis, split_axis=0, concat_axis=0, tiled=True)


def tables(cluster_pairs, my_index, groups):
    heads, clusters, _ = cluster_pairs.shape
    owned = clusters // groups
    by_group = cluster_pairs.reshape(heads, groups, owned * PAIRS)
    local = jnp.arange(owned, dtype=I32)
    earlier = (local[:, None] < local[None, :]).astype(F32)
    needed = jnp.any(by_group[:, :, None, :] == (my_index * owned + local)[None, None, :, None], axis=3)
    order = jnp.einsum("hac,cd->had", needed.astype(F32), earlier).astype(I32)
    hits = needed[:, :, None, :] & (order[:, :, None, :] == jnp.arange(KCAP, dtype=I32)[:, None])
    pick = jnp.sum(jnp.where(hits, local, 0), axis=3)
    own = lax.dynamic_index_in_dim(by_group, my_index, 1, keepdims=False)
    every = jnp.arange(clusters, dtype=I32)
    same = own[:, :, None] == every
    wanted = jnp.any(same, axis=1).reshape(heads, groups, owned)
    rank = jnp.einsum("hac,cd->had", wanted.astype(F32), earlier).astype(I32)
    position = (rank + jnp.arange(groups, dtype=I32)[None, :, None] * KCAP).reshape(heads, 1, clusters)
    fetch = jnp.sum(jnp.where(same, position, 0), axis=2)
    return pick, fetch.reshape(heads, owned, PAIRS)


def per_device(query_rows, key_rows, value_rows, query_cluster, key_cluster, cluster_pairs):
    heads, tokens = query_cluster.shape
    groups = lax.axis_size("seq")
    parts = lax.axis_size("head")
    my_index = lax.axis_index("seq")
    clusters = cluster_pairs.shape[1]
    owned = clusters // groups
    capacity = 3 * tokens // (2 * groups)
    slots = groups * capacity
    part = tokens // parts
    width = heads * LANES
    chunks = tokens // LANES

    most = heads - 1
    me = lax.axis_index("head").astype(I32).reshape(1)

    kv_sent = pl.pallas_call(
        split_kernel,
        grid=(4,),
        in_specs=[pl.BlockSpec((part // 4, parts * width), lambda i: (i, 0))] * 2,
        out_specs=pl.BlockSpec((parts, 2, part // 4, most * LANES), lambda i: (0, 0, i, 0)),
        out_shape=shape_of((parts, 2, part, most * LANES), BF16),
        compiler_params=params(),
        cost_estimate=cost(0, 6e6),
        name="split_kv",
    )(key_rows, value_rows)
    kv_tok = exchange(kv_sent, "head")
    last_parts = [shape_of((2, part, LANES), BF16)] * parts
    query_parts = [shape_of((part, width), BF16)] * parts
    pieces = pl.pallas_call(
        split_rest_kernel,
        grid_spec=pltpu.PrefetchScalarGridSpec(
            num_scalar_prefetch=1,
            grid=(2,),
            in_specs=[pl.BlockSpec((part // 2, parts * width), lambda i, me: (i, 0))] * 3,
            out_specs=[pl.BlockSpec((2, part // 2, LANES), lambda i, me: (0, i, 0))] * parts
            + [pl.BlockSpec((part // 2, width), lambda i, me: (i, 0))] * parts,
        ),
        out_shape=last_parts + query_parts,
        compiler_params=params(),
        cost_estimate=cost(0, 6e6),
        name="split_rest",
    )(me, key_rows, value_rows, query_rows)
    ids = jnp.concatenate([query_cluster, key_cluster], axis=0).reshape(2 * heads, chunks, LANES)
    slot, count = pl.pallas_call(
        functools.partial(slot_kernel, groups=groups, owned=owned, capacity=capacity),
        grid=(2 * heads,),
        in_specs=[pl.BlockSpec((1, chunks, LANES), lambda h: (h, 0, 0))],
        out_specs=[
            pl.BlockSpec((1, chunks, LANES), lambda h: (h, 0, 0)),
            pl.BlockSpec((1, groups, LANES), lambda h: (h, 0, 0)),
        ],
        out_shape=[
            shape_of((2 * heads, chunks, LANES), I32),
            shape_of((2 * heads, groups, LANES), F32),
        ],
        compiler_params=params(),
        cost_estimate=cost(2e9 * heads, 1e6),
        name="slots",
    )(ids)
    pick, fetch = tables(cluster_pairs, my_index, groups)

    *pieces, kv_tok = lax.optimization_barrier((*pieces, kv_tok))
    kv_packed = pl.pallas_call(
        pack_kv_kernel,
        grid=(most,),
        in_specs=[
            pl.BlockSpec((1, chunks, LANES), lambda h: (h + heads, 0, 0)),
            pl.BlockSpec((2 * heads, groups, LANES), lambda h: (0, 0, 0)),
            pl.BlockSpec((parts, 1, part, LANES), lambda h: (0, 0, 0, h)),
            pl.BlockSpec((parts, 1, part, LANES), lambda h: (0, 1, 0, h)),
        ],
        out_specs=pl.BlockSpec((groups, most * capacity + META, 2 * LANES), lambda h: (0, 0, 0)),
        out_shape=shape_of((groups, most * capacity + META, 2 * LANES), BF16),
        compiler_params=params(),
        cost_estimate=cost(most * 4.0 * slots * tokens * LANES, 8e6),
        name="pack_kv",
    )(slot, count, kv_tok, kv_tok)
    kv_recv = exchange(kv_packed, "seq")

    def to_partner(array, k):
        return lax.ppermute(array, "head", [(i, i ^ k) for i in range(parts)])

    *pieces, _ = lax.optimization_barrier((*pieces, kv_packed))
    last_tok = [to_partner(piece, k) if k else piece for k, piece in enumerate(pieces[:parts])]
    both = lax.optimization_barrier((*last_tok, *pieces[parts:]))
    last_tok, q_sent = both[:parts], both[parts:]
    q_tok = [to_partner(piece, k) if k else piece for k, piece in enumerate(q_sent)]

    last_packed = pl.pallas_call(
        pack_last_kernel,
        grid_spec=pltpu.PrefetchScalarGridSpec(
            num_scalar_prefetch=1,
            grid=(1,),
            in_specs=[pl.BlockSpec((1, chunks, LANES), lambda i, me: (2 * heads - 1, 0, 0))]
            + [pl.BlockSpec((2, part, LANES), lambda i, me: (0, 0, 0))] * parts,
            out_specs=pl.BlockSpec((groups, capacity, 2 * LANES), lambda i, me: (0, 0, 0)),
        ),
        out_shape=shape_of((groups, capacity, 2 * LANES), BF16),
        compiler_params=params(),
        cost_estimate=cost(4.0 * slots * tokens * LANES, 3e6),
        name="pack_last",
    )(me, slot, *last_tok)
    last_packed, kv_recv, *q_tok = lax.optimization_barrier((last_packed, kv_recv, *q_tok))
    last_kv_recv = exchange(last_packed, "seq")

    q_packed = pl.pallas_call(
        pack_q_kernel,
        grid_spec=pltpu.PrefetchScalarGridSpec(
            num_scalar_prefetch=1,
            grid=(heads,),
            in_specs=[pl.BlockSpec((1, chunks, LANES), lambda h, me: (h, 0, 0))]
            + [pl.BlockSpec((part, LANES), lambda h, me: (0, h))] * parts,
            out_specs=pl.BlockSpec((groups, 1, capacity, LANES), lambda h, me: (0, h, 0, 0)),
        ),
        out_shape=shape_of((groups, heads, capacity, LANES), BF16),
        compiler_params=params(),
        cost_estimate=cost(heads * 4.0 * slots * tokens * LANES, 4e6),
        name="pack_q",
    )(me, slot, *q_tok)
    q_packed, last_kv_recv = lax.optimization_barrier((q_packed, last_kv_recv))
    q_recv = exchange(q_packed, "seq")

    splits = ((0, heads - 1), (heads - 1, 1))
    block = (groups, 1, KCAP, BLOCK, 2 * LANES)
    first_sent, last_sent, index = pl.pallas_call(
        unpack_kv_kernel,
        grid_spec=pltpu.PrefetchScalarGridSpec(
            num_scalar_prefetch=1,
            grid=(heads,),
            in_specs=[
                pl.BlockSpec(
                    (groups, capacity, 2 * LANES), lambda h, pick: (0, jnp.minimum(h, most - 1), 0)
                ),
                pl.BlockSpec((groups, capacity, 2 * LANES), lambda h, pick: (0, 0, 0)),
                pl.BlockSpec(
                    (groups, META, 2 * LANES), lambda h, pick: (0, most * capacity // META, 0)
                ),
            ],
            out_specs=[
                pl.BlockSpec(block, lambda h, pick: (0, jnp.minimum(h, heads - 2), 0, 0, 0)),
                pl.BlockSpec(block, lambda h, pick: (0, 0, 0, 0, 0)),
                pl.BlockSpec((1, owned, BLOCK), lambda h, pick: (h, 0, 0)),
            ],
            scratch_shapes=[
                pltpu.VMEM((owned * BLOCK, LANES), I32),
                pltpu.VMEM((owned, BLOCK, 2 * LANES), BF16),
            ],
        ),
        out_shape=[
            shape_of((groups, heads - 1, KCAP, BLOCK, 2 * LANES), BF16),
            shape_of(block, BF16),
            shape_of((heads, owned, BLOCK), I32),
        ],
        compiler_params=params(),
        cost_estimate=cost(heads * 4.0 * slots * tokens * LANES, heads * 6e6),
        name="unpack_kv",
    )(pick, kv_recv, last_kv_recv, kv_recv)
    first_recv = exchange(first_sent, "seq")
    last_recv = exchange(last_sent, "seq")
    received = (first_recv, last_recv)
    q_recv, index, _ = lax.optimization_barrier((q_recv, index, first_recv))

    q_sorted = pl.pallas_call(
        unpack_q_kernel,
        grid=(heads,),
        in_specs=[
            pl.BlockSpec((1, owned, BLOCK), lambda h: (h, 0, 0)),
            pl.BlockSpec((groups, 1, capacity, LANES), lambda h: (0, h, 0, 0)),
        ],
        out_specs=pl.BlockSpec((1, owned * BLOCK, LANES), lambda h: (h, 0, 0)),
        out_shape=shape_of((heads, owned * BLOCK, LANES), BF16),
        scratch_shapes=[pltpu.VMEM((owned * BLOCK, LANES), I32)],
        compiler_params=params(),
        cost_estimate=cost(heads * 4.0 * slots * tokens * LANES, 4e6),
        name="unpack_q",
    )(index, q_recv)

    token_rows = None
    for (first, count_heads), recv in zip(splits, received, strict=True):
        reply = pl.pallas_call(
            functools.partial(attend_kernel, first=first),
            grid_spec=pltpu.PrefetchScalarGridSpec(
                num_scalar_prefetch=1,
                grid=(count_heads,),
                in_specs=[
                    pl.BlockSpec((1, owned, BLOCK), lambda h, fetch, first=first: (h + first, 0, 0)),
                    pl.BlockSpec(
                        (1, owned * BLOCK, LANES), lambda h, fetch, first=first: (h + first, 0, 0)
                    ),
                    pl.BlockSpec(
                        (groups, 1, KCAP, BLOCK, 2 * LANES), lambda h, fetch: (0, h, 0, 0, 0)
                    ),
                ],
                out_specs=pl.BlockSpec((groups, 1, capacity, LANES), lambda h, fetch: (0, h, 0, 0)),
                scratch_shapes=[pltpu.VMEM((owned * BLOCK, LANES), BF16)],
            ),
            out_shape=shape_of((groups, count_heads, capacity, LANES), BF16),
            compiler_params=params(),
            cost_estimate=cost(
                count_heads * 4.0 * owned * BLOCK * PAIRS * BLOCK * LANES,
                count_heads * 6e6,
                count_heads * owned * BLOCK * PAIRS * BLOCK,
            ),
            name=f"attend_{first}",
        )(fetch, index, q_sorted, recv)
        returned = exchange(reply, "seq")
        operands = (slot, returned) + (() if token_rows is None else (token_rows,))
        token_rows = pl.pallas_call(
            final_kernel,
            grid=(count_heads,),
            in_specs=[
                pl.BlockSpec((1, chunks, LANES), lambda h, first=first: (h + first, 0, 0)),
                pl.BlockSpec((groups, 1, capacity, LANES), lambda h: (0, h, 0, 0)),
            ]
            + [pl.BlockSpec(memory_space=pl.ANY)] * (len(operands) - 2),
            out_specs=pl.BlockSpec((parts, part, LANES), lambda h, first=first: (0, 0, h + first)),
            out_shape=shape_of((parts, part, width), BF16),
            scratch_shapes=[pltpu.VMEM((tokens, LANES), I32)],
            input_output_aliases={} if token_rows is None else {2: 0},
            compiler_params=params(),
            cost_estimate=cost(count_heads * 4.0 * slots * tokens * LANES, 2e6),
            name=f"final_{first}",
        )(*operands)
    rows = exchange(token_rows, "head")
    return rows.transpose(1, 0, 2).reshape(part, parts * width)


def solution(mesh):
    in_specs = (
        P(("seq", "head"), None),
        P(("seq", "head"), None),
        P(("seq", "head"), None),
        P("head", "seq"),
        P("head", "seq"),
        P("head", None, None),
    )
    out_specs = P(("seq", "head"), None)
    return jax.shard_map(
        per_device, mesh=mesh, in_specs=in_specs, out_specs=out_specs, check_vma=False
    )
```

```python
import functools
import math

import jax
import jax.numpy as jnp
from jax import lax
from jax.experimental import pallas as pl
from jax.experimental.pallas import tpu as pltpu
from jax.sharding import PartitionSpec as P

BLOCK = 128
PAIRS = 16
KCAP = 4
LANES = 128
META = 16
VMEM_LIMIT = 56 * 1024 * 1024
BF16 = jnp.bfloat16
F32 = jnp.float32
I32 = jnp.int32


def dot(left, right):
    return jnp.dot(left, right, preferred_element_type=F32)


def iota(shape, dim):
    return lax.broadcasted_iota(I32, shape, dim)


def params():
    return pltpu.CompilerParams(vmem_limit_bytes=VMEM_LIMIT)


def slot_kernel(ids_ref, slot_ref, count_ref, *, groups, owned, capacity):
    clusters = groups * owned
    chunks = ids_ref.shape[1]
    row = iota((clusters, LANES), 0)
    lane = iota((clusters, LANES), 1)
    before = iota((LANES, 2 * LANES), 0)
    after = iota((LANES, 2 * LANES), 1)
    running = ((after >= LANES) | (before <= after)).astype(BF16)
    every = jnp.ones((LANES, LANES), BF16)
    counts = jnp.zeros((clusters, LANES), F32)
    for chunk in range(chunks):
        hit = (ids_ref[0, chunk : chunk + 1, :] == row).astype(BF16)
        counts = counts + dot(hit, every)
    first = iota((clusters, clusters), 0)
    second = iota((clusters, clusters), 1)
    inside = ((second < first) & (second // owned == first // owned)).astype(BF16)
    carry = dot(inside, counts.astype(BF16)) + ((row // owned) * capacity - 1).astype(F32)
    own = jnp.where(lane == row % owned, counts, 0.0).astype(BF16)
    of_group = (iota((groups, clusters), 0) == iota((groups, clusters), 1) // owned).astype(BF16)
    count_ref[0] = dot(of_group, own)
    for chunk in range(chunks):
        match = ids_ref[0, chunk : chunk + 1, :] == row
        sums = dot(match.astype(BF16), running)
        picked = jnp.where(match, sums[:, :LANES] + carry, 0.0)
        slot_ref[0, chunk : chunk + 1, :] = jnp.sum(picked, axis=0, keepdims=True).astype(I32)
        carry = carry + sums[:, LANES:]


def spread(index, rows, store, slots, step):
    flat = jnp.concatenate([index[i : i + 1, :] for i in range(index.shape[0])], axis=1)
    count = flat.shape[1]
    within = iota((step, count), 0)

    def body(i, carry):
        onehot = (flat - i * step == within).astype(BF16)
        store(i, dot(onehot, rows).astype(BF16))
        return carry

    lax.fori_loop(0, slots // step, body, 0)


def collect(index, packed, wide_ref, store, step):
    turned = index.astype(F32).T
    chunks = index.shape[0]
    for i in range(chunks):
        wide_ref[i * LANES : (i + 1) * LANES, :] = jnp.broadcast_to(
            turned[:, i : i + 1], (LANES, LANES)
        ).astype(I32)
    lane = iota((step, LANES), 1)
    narrow = packed.shape[1] == LANES
    depth = packed.shape[0] // 2 if narrow else packed.shape[0]
    if narrow:
        packed = jnp.concatenate([packed[:depth], packed[depth:]], axis=1)

    def body(i, carry):
        wide = wide_ref[pl.ds(pl.multiple_of(i * step, step), step), :]
        second = wide >= depth
        if narrow:
            wide = jnp.where(second, wide - depth, wide)
        wide = wide - lane
        onehot = jnp.concatenate(
            [(wide == t * LANES).astype(BF16) for t in range(depth // LANES)], axis=1
        )
        block = dot(onehot, packed)
        if narrow:
            block = jnp.where(second, block[:, LANES:], block[:, :LANES])
        store(i, block.astype(BF16))
        return carry

    lax.fori_loop(0, chunks * LANES // step, body, 0)


def split_kernel(key_ref, value_ref, out_ref):
    parts, _, _, width = out_ref.shape
    stride = key_ref.shape[1] // parts
    for part in range(parts):
        columns = slice(part * stride, part * stride + width)
        out_ref[part, 0] = key_ref[:, columns]
        out_ref[part, 1] = value_ref[:, columns]


def split_rest_kernel(me_ref, key_ref, value_ref, query_ref, *out_refs):
    parts = len(out_refs) // 2
    stride = key_ref.shape[1] // parts
    me = me_ref[0]
    for k in range(parts):
        start = jnp.bitwise_xor(me, k) * stride
        last = pl.ds(pl.multiple_of(start + stride - LANES, LANES), LANES)
        out_refs[k][0] = key_ref[:, last]
        out_refs[k][1] = value_ref[:, last]
        out_refs[parts + k][...] = query_ref[:, pl.ds(pl.multiple_of(start, LANES), stride)]


def partner_order(me, index, parts):
    each = index.shape[0] // parts
    row = iota(index.shape, 0)
    rows = []
    for k in range(parts):
        for j in range(each):
            wanted = jnp.bitwise_xor(me, k) * each + j
            rows.append(jnp.sum(jnp.where(row == wanted, index, 0), axis=0, keepdims=True))
    return jnp.concatenate(rows, axis=0)


def pack_kv_kernel(slot_ref, count_ref, key_ref, value_ref, out_ref):
    head = pl.program_id(0)
    heads = pl.num_programs(0)
    groups, rows, _ = out_ref.shape
    of_heads = count_ref.shape[0] // 2
    capacity = (rows - META) // (of_heads - 1)
    tokens = key_ref.shape[0] * key_ref.shape[2]
    keys = key_ref[:, 0].reshape(tokens, LANES)
    values = value_ref[:, 0].reshape(tokens, LANES)
    at = pl.ds(pl.multiple_of(head * capacity, META), capacity)
    per = groups // 2

    def store(i, block):
        out_ref[pl.ds(per * i, per), at, :] = block.reshape(per, capacity, 2 * LANES)

    both = jnp.concatenate([keys, values], axis=1)
    spread(slot_ref[0], both, store, groups * capacity, per * capacity)

    @pl.when(head == heads - 1)
    def _():
        row = iota((groups, META, LANES), 1)
        for side in range(2):
            block = jnp.zeros((groups, META, LANES), F32)
            for h in range(of_heads):
                counts = count_ref[(1 - side) * of_heads + h]
                block = jnp.where(row == h, counts[:, None, :], block)
            out_ref[:, rows - META :, side * LANES : (side + 1) * LANES] = block.astype(BF16)


def pack_last_kernel(me_ref, slot_ref, *refs):
    *part_refs, out_ref = refs
    groups, capacity, _ = out_ref.shape
    index = partner_order(me_ref[0], slot_ref[0], len(part_refs))
    keys = jnp.concatenate([ref[0] for ref in part_refs], axis=0)
    values = jnp.concatenate([ref[1] for ref in part_refs], axis=0)
    per = groups // 2

    def store(i, block):
        out_ref[pl.ds(per * i, per)] = block.reshape(per, capacity, 2 * LANES)

    both = jnp.concatenate([keys, values], axis=1)
    spread(index, both, store, groups * capacity, per * capacity)


def pack_q_kernel(me_ref, slot_ref, *refs):
    *part_refs, out_ref = refs
    groups, _, capacity, _ = out_ref.shape
    index = partner_order(me_ref[0], slot_ref[0], len(part_refs))
    queries = jnp.concatenate([ref[...] for ref in part_refs], axis=0)
    per = groups // 2

    def store(i, block):
        out_ref[pl.ds(per * i, per), 0] = block.reshape(per, capacity, LANES)

    spread(index, queries, store, groups * capacity, per * capacity)


def sources(counts, capacity):
    groups = counts.shape[0]
    padded = jnp.concatenate([counts, jnp.zeros((LANES - groups, LANES), F32)], axis=0).astype(BF16)
    row = iota((LANES, LANES), 0)
    col = iota((LANES, LANES), 1)
    below = dot((col < row).astype(BF16), padded)
    offset = dot(padded, (row < col).astype(BF16))
    start = (row * capacity).astype(F32) + offset - below
    below_t = below.T[:groups]
    start_t = start.T[:groups]
    place = iota((groups, LANES), 1).astype(F32)
    found = jnp.broadcast_to(start_t[:, 0:1], (groups, LANES))
    for source in range(1, groups):
        found = jnp.where(below_t[:, source : source + 1] <= place, start_t[:, source : source + 1], found)
    return (found + place).astype(I32)


def unpack_kv_kernel(
    pick_ref,
    in_ref,
    last_in_ref,
    meta_ref,
    first_ref,
    last_ref,
    query_source_ref,
    wide_ref,
    sorted_ref,
):
    head = pl.program_id(0)
    heads = pl.num_programs(0)
    groups, capacity, _ = in_ref.shape
    row = iota(meta_ref.shape, 1)
    counts = jnp.sum(jnp.where(row == head, meta_ref[...].astype(F32), 0.0), axis=1)
    query_source_ref[0] = sources(counts[:, LANES:], capacity)
    key_source = sources(counts[:, :LANES], capacity)

    def store(i, block):
        sorted_ref[pl.ds(8 * i, 8)] = block.reshape(8, BLOCK, 2 * LANES)

    def send(packed_ref, out_ref):
        packed = packed_ref[...].reshape(groups * capacity, 2 * LANES)
        collect(key_source, packed, wide_ref, store, 8 * BLOCK)

        def copy(i, carry):
            for j in range(KCAP):
                out_ref[i, 0, j] = sorted_ref[pick_ref[head, i, j]]
            return carry

        lax.fori_loop(0, groups, copy, 0)

    @pl.when(head < heads - 1)
    def _():
        send(in_ref, first_ref)

    @pl.when(head == heads - 1)
    def _():
        send(last_in_ref, last_ref)


def unpack_q_kernel(index_ref, in_ref, out_ref, wide_ref):
    groups, _, capacity, _ = in_ref.shape
    packed = in_ref[:, 0].reshape(groups * capacity, LANES)
    step = 8 * BLOCK

    def store(i, block):
        out_ref[0, pl.ds(pl.multiple_of(i * step, step), step), :] = block

    collect(index_ref[0], packed, wide_ref, store, step)


def final_kernel(index_ref, in_ref, *refs):
    out_ref, wide_ref = refs[-2:]
    groups, _, capacity, _ = in_ref.shape
    packed = in_ref[:, 0].reshape(groups * capacity, LANES)
    part = out_ref.shape[1]

    def store(i, block):
        out_ref[pl.ds(4 * i, 4)] = block.reshape(4, part, LANES)

    collect(index_ref[0], packed, wide_ref, store, 4 * part)


def attend_kernel(fetch_ref, index_ref, query_ref, recv_ref, out_ref, attended_ref, *, first):
    head = pl.program_id(0) + first
    groups, _, capacity, _ = out_ref.shape
    owned = query_ref.shape[1] // BLOCK
    scale = math.log2(math.e) / math.sqrt(LANES)

    def one(cluster):
        rows = pl.ds(pl.multiple_of(cluster * BLOCK, BLOCK), BLOCK)
        queries = query_ref[0, rows, :]
        blocks = []
        for pair in range(PAIRS):
            at = fetch_ref[head, cluster, pair]
            blocks.append((at // KCAP, at % KCAP))
        keys = jnp.concatenate([recv_ref[b, 0, j, :, :LANES] for b, j in blocks], axis=0)
        values = jnp.concatenate([recv_ref[b, 0, j, :, LANES:] for b, j in blocks], axis=0)
        scores = lax.dot_general(
            queries, keys, (((1,), (1,)), ((), ())), preferred_element_type=F32
        )
        weights = jnp.exp2((scores - jnp.max(scores, axis=1, keepdims=True)) * scale)
        total = jnp.sum(weights, axis=1, keepdims=True)
        mixed = dot(weights.astype(BF16), values)
        attended_ref[rows, :] = (mixed / total).astype(BF16)

    def body(i, carry):
        for j in range(4):
            one(4 * i + j)
        return carry

    lax.fori_loop(0, owned // 4, body, 0)

    per = groups // 2

    def store(i, block):
        out_ref[pl.ds(per * i, per), 0] = block.reshape(per, capacity, LANES)

    spread(index_ref[0], attended_ref[...], store, groups * capacity, per * capacity)


def shape_of(shape, dtype):
    return jax.ShapeDtypeStruct(shape, dtype)


def cost(flops, moved, exps=0):
    return pl.CostEstimate(flops=int(flops), bytes_accessed=int(moved), transcendentals=int(exps))


def exchange(array, axis):
    return lax.all_to_all(array, axis, split_axis=0, concat_axis=0, tiled=True)


def tables(cluster_pairs, my_index, groups):
    heads, clusters, _ = cluster_pairs.shape
    owned = clusters // groups
    by_group = cluster_pairs.reshape(heads, groups, owned * PAIRS)
    local = jnp.arange(owned, dtype=I32)
    earlier = (local[:, None] < local[None, :]).astype(F32)
    needed = jnp.any(by_group[:, :, None, :] == (my_index * owned + local)[None, None, :, None], axis=3)
    order = jnp.einsum("hac,cd->had", needed.astype(F32), earlier).astype(I32)
    hits = needed[:, :, None, :] & (order[:, :, None, :] == jnp.arange(KCAP, dtype=I32)[:, None])
    pick = jnp.sum(jnp.where(hits, local, 0), axis=3)
    own = lax.dynamic_index_in_dim(by_group, my_index, 1, keepdims=False)
    every = jnp.arange(clusters, dtype=I32)
    same = own[:, :, None] == every
    wanted = jnp.any(same, axis=1).reshape(heads, groups, owned)
    rank = jnp.einsum("hac,cd->had", wanted.astype(F32), earlier).astype(I32)
    position = (rank + jnp.arange(groups, dtype=I32)[None, :, None] * KCAP).reshape(heads, 1, clusters)
    fetch = jnp.sum(jnp.where(same, position, 0), axis=2)
    return pick, fetch.reshape(heads, owned, PAIRS)


def per_device(query_rows, key_rows, value_rows, query_cluster, key_cluster, cluster_pairs):
    heads, tokens = query_cluster.shape
    groups = lax.axis_size("seq")
    parts = lax.axis_size("head")
    my_index = lax.axis_index("seq")
    clusters = cluster_pairs.shape[1]
    owned = clusters // groups
    capacity = 3 * tokens // (2 * groups)
    slots = groups * capacity
    part = tokens // parts
    width = heads * LANES
    chunks = tokens // LANES

    most = heads - 1
    me = lax.axis_index("head").astype(I32).reshape(1)

    kv_sent = pl.pallas_call(
        split_kernel,
        grid=(4,),
        in_specs=[pl.BlockSpec((part // 4, parts * width), lambda i: (i, 0))] * 2,
        out_specs=pl.BlockSpec((parts, 2, part // 4, most * LANES), lambda i: (0, 0, i, 0)),
        out_shape=shape_of((parts, 2, part, most * LANES), BF16),
        compiler_params=params(),
        cost_estimate=cost(0, 6e6),
        name="split_kv",
    )(key_rows, value_rows)
    kv_tok = exchange(kv_sent, "head")
    last_parts = [shape_of((2, part, LANES), BF16)] * parts
    query_parts = [shape_of((part, width), BF16)] * parts
    pieces = pl.pallas_call(
        split_rest_kernel,
        grid_spec=pltpu.PrefetchScalarGridSpec(
            num_scalar_prefetch=1,
            grid=(2,),
            in_specs=[pl.BlockSpec((part // 2, parts * width), lambda i, me: (i, 0))] * 3,
            out_specs=[pl.BlockSpec((2, part // 2, LANES), lambda i, me: (0, i, 0))] * parts
            + [pl.BlockSpec((part // 2, width), lambda i, me: (i, 0))] * parts,
        ),
        out_shape=last_parts + query_parts,
        compiler_params=params(),
        cost_estimate=cost(0, 6e6),
        name="split_rest",
    )(me, key_rows, value_rows, query_rows)
    ids = jnp.concatenate([query_cluster, key_cluster], axis=0).reshape(2 * heads, chunks, LANES)
    slot, count = pl.pallas_call(
        functools.partial(slot_kernel, groups=groups, owned=owned, capacity=capacity),
        grid=(2 * heads,),
        in_specs=[pl.BlockSpec((1, chunks, LANES), lambda h: (h, 0, 0))],
        out_specs=[
            pl.BlockSpec((1, chunks, LANES), lambda h: (h, 0, 0)),
            pl.BlockSpec((1, groups, LANES), lambda h: (h, 0, 0)),
        ],
        out_shape=[
            shape_of((2 * heads, chunks, LANES), I32),
            shape_of((2 * heads, groups, LANES), F32),
        ],
        compiler_params=params(),
        cost_estimate=cost(2e9 * heads, 1e6),
        name="slots",
    )(ids)
    pick, fetch = tables(cluster_pairs, my_index, groups)

    *pieces, kv_tok = lax.optimization_barrier((*pieces, kv_tok))
    kv_packed = pl.pallas_call(
        pack_kv_kernel,
        grid=(most,),
        in_specs=[
            pl.BlockSpec((1, chunks, LANES), lambda h: (h + heads, 0, 0)),
            pl.BlockSpec((2 * heads, groups, LANES), lambda h: (0, 0, 0)),
            pl.BlockSpec((parts, 1, part, LANES), lambda h: (0, 0, 0, h)),
            pl.BlockSpec((parts, 1, part, LANES), lambda h: (0, 1, 0, h)),
        ],
        out_specs=pl.BlockSpec((groups, most * capacity + META, 2 * LANES), lambda h: (0, 0, 0)),
        out_shape=shape_of((groups, most * capacity + META, 2 * LANES), BF16),
        compiler_params=params(),
        cost_estimate=cost(most * 4.0 * slots * tokens * LANES, 8e6),
        name="pack_kv",
    )(slot, count, kv_tok, kv_tok)
    kv_recv = exchange(kv_packed, "seq")

    def to_partner(array, k):
        return lax.ppermute(array, "head", [(i, i ^ k) for i in range(parts)])

    *pieces, _ = lax.optimization_barrier((*pieces, kv_packed))
    last_tok = [to_partner(piece, k) if k else piece for k, piece in enumerate(pieces[:parts])]
    both = lax.optimization_barrier((*last_tok, *pieces[parts:]))
    last_tok, q_sent = both[:parts], both[parts:]
    q_tok = [to_partner(piece, k) if k else piece for k, piece in enumerate(q_sent)]

    last_packed = pl.pallas_call(
        pack_last_kernel,
        grid_spec=pltpu.PrefetchScalarGridSpec(
            num_scalar_prefetch=1,
            grid=(1,),
            in_specs=[pl.BlockSpec((1, chunks, LANES), lambda i, me: (2 * heads - 1, 0, 0))]
            + [pl.BlockSpec((2, part, LANES), lambda i, me: (0, 0, 0))] * parts,
            out_specs=pl.BlockSpec((groups, capacity, 2 * LANES), lambda i, me: (0, 0, 0)),
        ),
        out_shape=shape_of((groups, capacity, 2 * LANES), BF16),
        compiler_params=params(),
        cost_estimate=cost(4.0 * slots * tokens * LANES, 3e6),
        name="pack_last",
    )(me, slot, *last_tok)
    last_packed, kv_recv, *q_tok = lax.optimization_barrier((last_packed, kv_recv, *q_tok))
    last_kv_recv = exchange(last_packed, "seq")

    q_packed = pl.pallas_call(
        pack_q_kernel,
        grid_spec=pltpu.PrefetchScalarGridSpec(
            num_scalar_prefetch=1,
            grid=(heads,),
            in_specs=[pl.BlockSpec((1, chunks, LANES), lambda h, me: (h, 0, 0))]
            + [pl.BlockSpec((part, LANES), lambda h, me: (0, h))] * parts,
            out_specs=pl.BlockSpec((groups, 1, capacity, LANES), lambda h, me: (0, h, 0, 0)),
        ),
        out_shape=shape_of((groups, heads, capacity, LANES), BF16),
        compiler_params=params(),
        cost_estimate=cost(heads * 4.0 * slots * tokens * LANES, 4e6),
        name="pack_q",
    )(me, slot, *q_tok)
    q_packed, last_kv_recv = lax.optimization_barrier((q_packed, last_kv_recv))
    q_recv = exchange(q_packed, "seq")

    splits = ((0, heads - 1), (heads - 1, 1))
    block = (groups, 1, KCAP, BLOCK, 2 * LANES)
    first_sent, last_sent, index = pl.pallas_call(
        unpack_kv_kernel,
        grid_spec=pltpu.PrefetchScalarGridSpec(
            num_scalar_prefetch=1,
            grid=(heads,),
            in_specs=[
                pl.BlockSpec(
                    (groups, capacity, 2 * LANES), lambda h, pick: (0, jnp.minimum(h, most - 1), 0)
                ),
                pl.BlockSpec((groups, capacity, 2 * LANES), lambda h, pick: (0, 0, 0)),
                pl.BlockSpec(
                    (groups, META, 2 * LANES), lambda h, pick: (0, most * capacity // META, 0)
                ),
            ],
            out_specs=[
                pl.BlockSpec(block, lambda h, pick: (0, jnp.minimum(h, heads - 2), 0, 0, 0)),
                pl.BlockSpec(block, lambda h, pick: (0, 0, 0, 0, 0)),
                pl.BlockSpec((1, owned, BLOCK), lambda h, pick: (h, 0, 0)),
            ],
            scratch_shapes=[
                pltpu.VMEM((owned * BLOCK, LANES), I32),
                pltpu.VMEM((owned, BLOCK, 2 * LANES), BF16),
            ],
        ),
        out_shape=[
            shape_of((groups, heads - 1, KCAP, BLOCK, 2 * LANES), BF16),
            shape_of(block, BF16),
            shape_of((heads, owned, BLOCK), I32),
        ],
        compiler_params=params(),
        cost_estimate=cost(heads * 4.0 * slots * tokens * LANES, heads * 6e6),
        name="unpack_kv",
    )(pick, kv_recv, last_kv_recv, kv_recv)
    first_recv = exchange(first_sent, "seq")
    last_recv = exchange(last_sent, "seq")
    received = (first_recv, last_recv)
    q_recv, index, _ = lax.optimization_barrier((q_recv, index, first_recv))

    q_sorted = pl.pallas_call(
        unpack_q_kernel,
        grid=(heads,),
        in_specs=[
            pl.BlockSpec((1, owned, BLOCK), lambda h: (h, 0, 0)),
            pl.BlockSpec((groups, 1, capacity, LANES), lambda h: (0, h, 0, 0)),
        ],
        out_specs=pl.BlockSpec((1, owned * BLOCK, LANES), lambda h: (h, 0, 0)),
        out_shape=shape_of((heads, owned * BLOCK, LANES), BF16),
        scratch_shapes=[pltpu.VMEM((owned * BLOCK, LANES), I32)],
        compiler_params=params(),
        cost_estimate=cost(heads * 4.0 * slots * tokens * LANES, 4e6),
        name="unpack_q",
    )(index, q_recv)

    token_rows = None
    for (first, count_heads), recv in zip(splits, received, strict=True):
        reply = pl.pallas_call(
            functools.partial(attend_kernel, first=first),
            grid_spec=pltpu.PrefetchScalarGridSpec(
                num_scalar_prefetch=1,
                grid=(count_heads,),
                in_specs=[
                    pl.BlockSpec((1, owned, BLOCK), lambda h, fetch, first=first: (h + first, 0, 0)),
                    pl.BlockSpec(
                        (1, owned * BLOCK, LANES), lambda h, fetch, first=first: (h + first, 0, 0)
                    ),
                    pl.BlockSpec(
                        (groups, 1, KCAP, BLOCK, 2 * LANES), lambda h, fetch: (0, h, 0, 0, 0)
                    ),
                ],
                out_specs=pl.BlockSpec((groups, 1, capacity, LANES), lambda h, fetch: (0, h, 0, 0)),
                scratch_shapes=[pltpu.VMEM((owned * BLOCK, LANES), BF16)],
            ),
            out_shape=shape_of((groups, count_heads, capacity, LANES), BF16),
            compiler_params=params(),
            cost_estimate=cost(
                count_heads * 4.0 * owned * BLOCK * PAIRS * BLOCK * LANES,
                count_heads * 6e6,
                count_heads * owned * BLOCK * PAIRS * BLOCK,
            ),
            name=f"attend_{first}",
        )(fetch, index, q_sorted, recv)
        returned = exchange(reply, "seq")
        operands = (slot, returned) + (() if token_rows is None else (token_rows,))
        token_rows = pl.pallas_call(
            final_kernel,
            grid=(count_heads,),
            in_specs=[
                pl.BlockSpec((1, chunks, LANES), lambda h, first=first: (h + first, 0, 0)),
                pl.BlockSpec((groups, 1, capacity, LANES), lambda h: (0, h, 0, 0)),
            ]
            + [pl.BlockSpec(memory_space=pl.ANY)] * (len(operands) - 2),
            out_specs=pl.BlockSpec((parts, part, LANES), lambda h, first=first: (0, 0, h + first)),
            out_shape=shape_of((parts, part, width), BF16),
            scratch_shapes=[pltpu.VMEM((tokens, LANES), I32)],
            input_output_aliases={} if token_rows is None else {2: 0},
            compiler_params=params(),
            cost_estimate=cost(count_heads * 4.0 * slots * tokens * LANES, 2e6),
            name=f"final_{first}",
        )(*operands)
    rows = exchange(token_rows, "head")
    return rows.transpose(1, 0, 2).reshape(part, parts * width)


def solution(mesh):
    in_specs = (
        P(("seq", "head"), None),
        P(("seq", "head"), None),
        P(("seq", "head"), None),
        P("head", "seq"),
        P("head", "seq"),
        P("head", None, None),
    )
    out_specs = P(("seq", "head"), None)
    return jax.shard_map(
        per_device, mesh=mesh, in_specs=in_specs, out_specs=out_specs, check_vma=False
    )
```

```python
import functools
import math

import jax
import jax.numpy as jnp
from jax import lax
from jax.experimental import pallas as pl
from jax.experimental.pallas import tpu as pltpu
from jax.sharding import PartitionSpec as P

BLOCK = 128
PAIRS = 16
KCAP = 4
LANES = 128
META = 16
VMEM_LIMIT = 63 * 1024 * 1024
BF16 = jnp.bfloat16
F32 = jnp.float32
I32 = jnp.int32


def dot(left, right):
    return jnp.dot(left, right, preferred_element_type=F32)


def iota(shape, dim):
    return lax.broadcasted_iota(I32, shape, dim)


def params():
    return pltpu.CompilerParams(vmem_limit_bytes=VMEM_LIMIT)


def slot_kernel(ids_ref, slot_ref, count_ref, *, groups, owned, capacity):
    clusters = groups * owned
    chunks = ids_ref.shape[1]
    row = iota((clusters, LANES), 0)
    lane = iota((clusters, LANES), 1)
    before = iota((LANES, 2 * LANES), 0)
    after = iota((LANES, 2 * LANES), 1)
    running = ((after >= LANES) | (before <= after)).astype(BF16)
    every = jnp.ones((LANES, LANES), BF16)
    counts = jnp.zeros((clusters, LANES), F32)
    for chunk in range(chunks):
        hit = (ids_ref[0, chunk : chunk + 1, :] == row).astype(BF16)
        counts = counts + dot(hit, every)
    first = iota((clusters, clusters), 0)
    second = iota((clusters, clusters), 1)
    inside = ((second < first) & (second // owned == first // owned)).astype(BF16)
    carry = dot(inside, counts.astype(BF16)) + ((row // owned) * capacity - 1).astype(F32)
    own = jnp.where(lane == row % owned, counts, 0.0).astype(BF16)
    of_group = (iota((groups, clusters), 0) == iota((groups, clusters), 1) // owned).astype(BF16)
    count_ref[0] = dot(of_group, own)
    for chunk in range(chunks):
        match = ids_ref[0, chunk : chunk + 1, :] == row
        sums = dot(match.astype(BF16), running)
        picked = jnp.where(match, sums[:, :LANES] + carry, 0.0)
        slot_ref[0, chunk : chunk + 1, :] = jnp.sum(picked, axis=0, keepdims=True).astype(I32)
        carry = carry + sums[:, LANES:]


def spread(index, rows, store, slots, step):
    flat = jnp.concatenate([index[i : i + 1, :] for i in range(index.shape[0])], axis=1)
    count = flat.shape[1]
    within = iota((step, count), 0)

    def body(i, carry):
        onehot = (flat - i * step == within).astype(BF16)
        store(i, dot(onehot, rows).astype(BF16))
        return carry

    lax.fori_loop(0, slots // step, body, 0)


def collect(index, packed, wide_ref, store, step):
    turned = index.astype(F32).T
    chunks = index.shape[0]
    for i in range(chunks):
        wide_ref[i * LANES : (i + 1) * LANES, :] = jnp.broadcast_to(
            turned[:, i : i + 1], (LANES, LANES)
        ).astype(I32)
    lane = iota((step, LANES), 1)
    narrow = packed.shape[1] == LANES
    depth = packed.shape[0] // 2 if narrow else packed.shape[0]
    if narrow:
        packed = jnp.concatenate([packed[:depth], packed[depth:]], axis=1)

    def body(i, carry):
        wide = wide_ref[pl.ds(pl.multiple_of(i * step, step), step), :]
        second = wide >= depth
        if narrow:
            wide = jnp.where(second, wide - depth, wide)
        wide = wide - lane
        onehot = jnp.concatenate(
            [(wide == t * LANES).astype(BF16) for t in range(depth // LANES)], axis=1
        )
        block = dot(onehot, packed)
        if narrow:
            block = jnp.where(second, block[:, LANES:], block[:, :LANES])
        store(i, block.astype(BF16))
        return carry

    lax.fori_loop(0, chunks * LANES // step, body, 0)


def split_kernel(key_ref, value_ref, out_ref):
    parts, _, _, width = out_ref.shape
    stride = key_ref.shape[1] // parts
    for part in range(parts):
        columns = slice(part * stride, part * stride + width)
        out_ref[part, 0] = key_ref[:, columns]
        out_ref[part, 1] = value_ref[:, columns]


def split_rest_kernel(me_ref, key_ref, value_ref, query_ref, *out_refs):
    parts = len(out_refs) // 2
    stride = key_ref.shape[1] // parts
    me = me_ref[0]
    for k in range(parts):
        start = jnp.bitwise_xor(me, k) * stride
        last = pl.ds(pl.multiple_of(start + stride - LANES, LANES), LANES)
        out_refs[k][0] = key_ref[:, last]
        out_refs[k][1] = value_ref[:, last]
        out_refs[parts + k][...] = query_ref[:, pl.ds(pl.multiple_of(start, LANES), stride)]


def partner_order(me, index, parts):
    each = index.shape[0] // parts
    row = iota(index.shape, 0)
    rows = []
    for k in range(parts):
        for j in range(each):
            wanted = jnp.bitwise_xor(me, k) * each + j
            rows.append(jnp.sum(jnp.where(row == wanted, index, 0), axis=0, keepdims=True))
    return jnp.concatenate(rows, axis=0)


def pack_kv_kernel(slot_ref, count_ref, key_ref, value_ref, out_ref):
    head = pl.program_id(0)
    heads = pl.num_programs(0)
    groups, rows, _ = out_ref.shape
    of_heads = count_ref.shape[0] // 2
    capacity = (rows - META) // (of_heads - 1)
    tokens = key_ref.shape[0] * key_ref.shape[2]
    keys = key_ref[:, 0].reshape(tokens, LANES)
    values = value_ref[:, 0].reshape(tokens, LANES)
    at = pl.ds(pl.multiple_of(head * capacity, META), capacity)
    per = groups // 2

    def store(i, block):
        out_ref[pl.ds(per * i, per), at, :] = block.reshape(per, capacity, 2 * LANES)

    both = jnp.concatenate([keys, values], axis=1)
    spread(slot_ref[0], both, store, groups * capacity, per * capacity)

    @pl.when(head == heads - 1)
    def _():
        row = iota((groups, META, LANES), 1)
        for side in range(2):
            block = jnp.zeros((groups, META, LANES), F32)
            for h in range(of_heads):
                counts = count_ref[(1 - side) * of_heads + h]
                block = jnp.where(row == h, counts[:, None, :], block)
            out_ref[:, rows - META :, side * LANES : (side + 1) * LANES] = block.astype(BF16)


def pack_last_kernel(me_ref, slot_ref, *refs):
    *part_refs, out_ref = refs
    groups, capacity, _ = out_ref.shape
    index = partner_order(me_ref[0], slot_ref[0], len(part_refs))
    keys = jnp.concatenate([ref[0] for ref in part_refs], axis=0)
    values = jnp.concatenate([ref[1] for ref in part_refs], axis=0)
    per = groups // 2

    def store(i, block):
        out_ref[pl.ds(per * i, per)] = block.reshape(per, capacity, 2 * LANES)

    both = jnp.concatenate([keys, values], axis=1)
    spread(index, both, store, groups * capacity, per * capacity)


def pack_q_kernel(me_ref, slot_ref, *refs):
    *part_refs, out_ref = refs
    groups, _, capacity, _ = out_ref.shape
    index = partner_order(me_ref[0], slot_ref[0], len(part_refs))
    queries = jnp.concatenate([ref[...] for ref in part_refs], axis=0)
    per = groups // 2

    def store(i, block):
        out_ref[pl.ds(per * i, per), 0] = block.reshape(per, capacity, LANES)

    spread(index, queries, store, groups * capacity, per * capacity)


def sources(counts, capacity):
    groups = counts.shape[0]
    padded = jnp.concatenate([counts, jnp.zeros((LANES - groups, LANES), F32)], axis=0).astype(BF16)
    row = iota((LANES, LANES), 0)
    col = iota((LANES, LANES), 1)
    below = dot((col < row).astype(BF16), padded)
    offset = dot(padded, (row < col).astype(BF16))
    start = (row * capacity).astype(F32) + offset - below
    below_t = below.T[:groups]
    start_t = start.T[:groups]
    place = iota((groups, LANES), 1).astype(F32)
    found = jnp.broadcast_to(start_t[:, 0:1], (groups, LANES))
    for source in range(1, groups):
        found = jnp.where(below_t[:, source : source + 1] <= place, start_t[:, source : source + 1], found)
    return (found + place).astype(I32)


def unpack_kv_kernel(
    pick_ref,
    in_ref,
    last_in_ref,
    meta_ref,
    first_ref,
    last_ref,
    query_source_ref,
    wide_ref,
    sorted_ref,
):
    head = pl.program_id(0)
    heads = pl.num_programs(0)
    groups, capacity, _ = in_ref.shape
    row = iota(meta_ref.shape, 1)
    counts = jnp.sum(jnp.where(row == head, meta_ref[...].astype(F32), 0.0), axis=1)
    query_source_ref[0] = sources(counts[:, LANES:], capacity)
    key_source = sources(counts[:, :LANES], capacity)

    def store(i, block):
        sorted_ref[pl.ds(8 * i, 8)] = block.reshape(8, BLOCK, 2 * LANES)

    def send(packed_ref, out_ref):
        packed = packed_ref[...].reshape(groups * capacity, 2 * LANES)
        collect(key_source, packed, wide_ref, store, 8 * BLOCK)

        def copy(i, carry):
            for j in range(KCAP):
                out_ref[i, 0, j] = sorted_ref[pick_ref[head, i, j]]
            return carry

        lax.fori_loop(0, groups, copy, 0)

    @pl.when(head < heads - 1)
    def _():
        send(in_ref, first_ref)

    @pl.when(head == heads - 1)
    def _():
        send(last_in_ref, last_ref)


def unpack_q_kernel(index_ref, in_ref, out_ref, wide_ref):
    groups, _, capacity, _ = in_ref.shape
    packed = in_ref[:, 0].reshape(groups * capacity, LANES)
    step = 8 * BLOCK

    def store(i, block):
        out_ref[0, pl.ds(pl.multiple_of(i * step, step), step), :] = block

    collect(index_ref[0], packed, wide_ref, store, step)


def final_kernel(index_ref, in_ref, *refs):
    out_ref, wide_ref = refs[-2:]
    groups, _, capacity, _ = in_ref.shape
    packed = in_ref[:, 0].reshape(groups * capacity, LANES)
    part = out_ref.shape[1]

    def store(i, block):
        out_ref[pl.ds(4 * i, 4)] = block.reshape(4, part, LANES)

    collect(index_ref[0], packed, wide_ref, store, 4 * part)


def attend_kernel(fetch_ref, index_ref, query_ref, recv_ref, out_ref, attended_ref, *, first):
    head = pl.program_id(0) + first
    groups, _, capacity, _ = out_ref.shape
    owned = query_ref.shape[1] // BLOCK
    scale = math.log2(math.e) / math.sqrt(LANES)

    def one(cluster):
        rows = pl.ds(pl.multiple_of(cluster * BLOCK, BLOCK), BLOCK)
        queries = query_ref[0, rows, :]
        blocks = []
        for pair in range(PAIRS):
            at = fetch_ref[head, cluster, pair]
            blocks.append((at // KCAP, at % KCAP))
        keys = jnp.concatenate([recv_ref[b, 0, j, :, :LANES] for b, j in blocks], axis=0)
        values = jnp.concatenate([recv_ref[b, 0, j, :, LANES:] for b, j in blocks], axis=0)
        scores = lax.dot_general(
            queries, keys, (((1,), (1,)), ((), ())), preferred_element_type=F32
        )
        weights = jnp.exp2((scores - jnp.max(scores, axis=1, keepdims=True)) * scale)
        total = jnp.sum(weights, axis=1, keepdims=True)
        mixed = dot(weights.astype(BF16), values)
        attended_ref[rows, :] = (mixed / total).astype(BF16)

    def body(i, carry):
        for j in range(4):
            one(4 * i + j)
        return carry

    lax.fori_loop(0, owned // 4, body, 0)

    per = groups // 2

    def store(i, block):
        out_ref[pl.ds(per * i, per), 0] = block.reshape(per, capacity, LANES)

    spread(index_ref[0], attended_ref[...], store, groups * capacity, per * capacity)


def shape_of(shape, dtype):
    return jax.ShapeDtypeStruct(shape, dtype)


def cost(flops, moved, exps=0):
    return pl.CostEstimate(flops=int(flops), bytes_accessed=int(moved), transcendentals=int(exps))


def exchange(array, axis):
    return lax.all_to_all(array, axis, split_axis=0, concat_axis=0, tiled=True)


def tables(cluster_pairs, my_index, groups):
    heads, clusters, _ = cluster_pairs.shape
    owned = clusters // groups
    by_group = cluster_pairs.reshape(heads, groups, owned * PAIRS)
    local = jnp.arange(owned, dtype=I32)
    earlier = (local[:, None] < local[None, :]).astype(F32)
    needed = jnp.any(by_group[:, :, None, :] == (my_index * owned + local)[None, None, :, None], axis=3)
    order = jnp.einsum("hac,cd->had", needed.astype(F32), earlier).astype(I32)
    hits = needed[:, :, None, :] & (order[:, :, None, :] == jnp.arange(KCAP, dtype=I32)[:, None])
    pick = jnp.sum(jnp.where(hits, local, 0), axis=3)
    own = lax.dynamic_index_in_dim(by_group, my_index, 1, keepdims=False)
    every = jnp.arange(clusters, dtype=I32)
    same = own[:, :, None] == every
    wanted = jnp.any(same, axis=1).reshape(heads, groups, owned)
    rank = jnp.einsum("hac,cd->had", wanted.astype(F32), earlier).astype(I32)
    position = (rank + jnp.arange(groups, dtype=I32)[None, :, None] * KCAP).reshape(heads, 1, clusters)
    fetch = jnp.sum(jnp.where(same, position, 0), axis=2)
    return pick, fetch.reshape(heads, owned, PAIRS)


def per_device(query_rows, key_rows, value_rows, query_cluster, key_cluster, cluster_pairs):
    heads, tokens = query_cluster.shape
    groups = lax.axis_size("seq")
    parts = lax.axis_size("head")
    my_index = lax.axis_index("seq")
    clusters = cluster_pairs.shape[1]
    owned = clusters // groups
    capacity = 3 * tokens // (2 * groups)
    slots = groups * capacity
    part = tokens // parts
    width = heads * LANES
    chunks = tokens // LANES

    most = heads - 1
    me = lax.axis_index("head").astype(I32).reshape(1)

    kv_sent = pl.pallas_call(
        split_kernel,
        grid=(4,),
        in_specs=[pl.BlockSpec((part // 4, parts * width), lambda i: (i, 0))] * 2,
        out_specs=pl.BlockSpec((parts, 2, part // 4, most * LANES), lambda i: (0, 0, i, 0)),
        out_shape=shape_of((parts, 2, part, most * LANES), BF16),
        compiler_params=params(),
        cost_estimate=cost(0, 6e6),
        name="split_kv",
    )(key_rows, value_rows)
    kv_tok = exchange(kv_sent, "head")
    last_parts = [shape_of((2, part, LANES), BF16)] * parts
    query_parts = [shape_of((part, width), BF16)] * parts
    pieces = pl.pallas_call(
        split_rest_kernel,
        grid_spec=pltpu.PrefetchScalarGridSpec(
            num_scalar_prefetch=1,
            grid=(2,),
            in_specs=[pl.BlockSpec((part // 2, parts * width), lambda i, me: (i, 0))] * 3,
            out_specs=[pl.BlockSpec((2, part // 2, LANES), lambda i, me: (0, i, 0))] * parts
            + [pl.BlockSpec((part // 2, width), lambda i, me: (i, 0))] * parts,
        ),
        out_shape=last_parts + query_parts,
        compiler_params=params(),
        cost_estimate=cost(0, 6e6),
        name="split_rest",
    )(me, key_rows, value_rows, query_rows)
    ids = jnp.concatenate([query_cluster, key_cluster], axis=0).reshape(2 * heads, chunks, LANES)
    slot, count = pl.pallas_call(
        functools.partial(slot_kernel, groups=groups, owned=owned, capacity=capacity),
        grid=(2 * heads,),
        in_specs=[pl.BlockSpec((1, chunks, LANES), lambda h: (h, 0, 0))],
        out_specs=[
            pl.BlockSpec((1, chunks, LANES), lambda h: (h, 0, 0)),
            pl.BlockSpec((1, groups, LANES), lambda h: (h, 0, 0)),
        ],
        out_shape=[
            shape_of((2 * heads, chunks, LANES), I32),
            shape_of((2 * heads, groups, LANES), F32),
        ],
        compiler_params=params(),
        cost_estimate=cost(2e9 * heads, 1e6),
        name="slots",
    )(ids)
    pick, fetch = tables(cluster_pairs, my_index, groups)

    *pieces, kv_tok = lax.optimization_barrier((*pieces, kv_tok))
    kv_packed = pl.pallas_call(
        pack_kv_kernel,
        grid=(most,),
        in_specs=[
            pl.BlockSpec((1, chunks, LANES), lambda h: (h + heads, 0, 0)),
            pl.BlockSpec((2 * heads, groups, LANES), lambda h: (0, 0, 0)),
            pl.BlockSpec((parts, 1, part, LANES), lambda h: (0, 0, 0, h)),
            pl.BlockSpec((parts, 1, part, LANES), lambda h: (0, 1, 0, h)),
        ],
        out_specs=pl.BlockSpec((groups, most * capacity + META, 2 * LANES), lambda h: (0, 0, 0)),
        out_shape=shape_of((groups, most * capacity + META, 2 * LANES), BF16),
        compiler_params=params(),
        cost_estimate=cost(most * 4.0 * slots * tokens * LANES, 8e6),
        name="pack_kv",
    )(slot, count, kv_tok, kv_tok)
    kv_recv = exchange(kv_packed, "seq")

    def to_partner(array, k):
        return lax.ppermute(array, "head", [(i, i ^ k) for i in range(parts)])

    *pieces, _ = lax.optimization_barrier((*pieces, kv_packed))
    last_tok = [to_partner(piece, k) if k else piece for k, piece in enumerate(pieces[:parts])]
    both = lax.optimization_barrier((*last_tok, *pieces[parts:]))
    last_tok, q_sent = both[:parts], both[parts:]
    q_tok = [to_partner(piece, k) if k else piece for k, piece in enumerate(q_sent)]

    last_packed = pl.pallas_call(
        pack_last_kernel,
        grid_spec=pltpu.PrefetchScalarGridSpec(
            num_scalar_prefetch=1,
            grid=(1,),
            in_specs=[pl.BlockSpec((1, chunks, LANES), lambda i, me: (2 * heads - 1, 0, 0))]
            + [pl.BlockSpec((2, part, LANES), lambda i, me: (0, 0, 0))] * parts,
            out_specs=pl.BlockSpec((groups, capacity, 2 * LANES), lambda i, me: (0, 0, 0)),
        ),
        out_shape=shape_of((groups, capacity, 2 * LANES), BF16),
        compiler_params=params(),
        cost_estimate=cost(4.0 * slots * tokens * LANES, 3e6),
        name="pack_last",
    )(me, slot, *last_tok)
    last_packed, kv_recv, *q_tok = lax.optimization_barrier((last_packed, kv_recv, *q_tok))
    last_kv_recv = exchange(last_packed, "seq")

    q_packed = pl.pallas_call(
        pack_q_kernel,
        grid_spec=pltpu.PrefetchScalarGridSpec(
            num_scalar_prefetch=1,
            grid=(heads,),
            in_specs=[pl.BlockSpec((1, chunks, LANES), lambda h, me: (h, 0, 0))]
            + [pl.BlockSpec((part, LANES), lambda h, me: (0, h))] * parts,
            out_specs=pl.BlockSpec((groups, 1, capacity, LANES), lambda h, me: (0, h, 0, 0)),
        ),
        out_shape=shape_of((groups, heads, capacity, LANES), BF16),
        compiler_params=params(),
        cost_estimate=cost(heads * 4.0 * slots * tokens * LANES, 4e6),
        name="pack_q",
    )(me, slot, *q_tok)
    q_packed, last_kv_recv = lax.optimization_barrier((q_packed, last_kv_recv))
    q_recv = exchange(q_packed, "seq")

    splits = ((0, heads - 1), (heads - 1, 1))
    block = (groups, 1, KCAP, BLOCK, 2 * LANES)
    first_sent, last_sent, index = pl.pallas_call(
        unpack_kv_kernel,
        grid_spec=pltpu.PrefetchScalarGridSpec(
            num_scalar_prefetch=1,
            grid=(heads,),
            in_specs=[
                pl.BlockSpec(
                    (groups, capacity, 2 * LANES), lambda h, pick: (0, jnp.minimum(h, most - 1), 0)
                ),
                pl.BlockSpec((groups, capacity, 2 * LANES), lambda h, pick: (0, 0, 0)),
                pl.BlockSpec(
                    (groups, META, 2 * LANES), lambda h, pick: (0, most * capacity // META, 0)
                ),
            ],
            out_specs=[
                pl.BlockSpec(block, lambda h, pick: (0, jnp.minimum(h, heads - 2), 0, 0, 0)),
                pl.BlockSpec(block, lambda h, pick: (0, 0, 0, 0, 0)),
                pl.BlockSpec((1, owned, BLOCK), lambda h, pick: (h, 0, 0)),
            ],
            scratch_shapes=[
                pltpu.VMEM((owned * BLOCK, LANES), I32),
                pltpu.VMEM((owned, BLOCK, 2 * LANES), BF16),
            ],
        ),
        out_shape=[
            shape_of((groups, heads - 1, KCAP, BLOCK, 2 * LANES), BF16),
            shape_of(block, BF16),
            shape_of((heads, owned, BLOCK), I32),
        ],
        compiler_params=params(),
        cost_estimate=cost(heads * 4.0 * slots * tokens * LANES, heads * 6e6),
        name="unpack_kv",
    )(pick, kv_recv, last_kv_recv, kv_recv)
    first_recv = exchange(first_sent, "seq")
    last_recv = exchange(last_sent, "seq")
    received = (first_recv, last_recv)
    q_recv, index, _ = lax.optimization_barrier((q_recv, index, first_recv))

    q_sorted = pl.pallas_call(
        unpack_q_kernel,
        grid=(heads,),
        in_specs=[
            pl.BlockSpec((1, owned, BLOCK), lambda h: (h, 0, 0)),
            pl.BlockSpec((groups, 1, capacity, LANES), lambda h: (0, h, 0, 0)),
        ],
        out_specs=pl.BlockSpec((1, owned * BLOCK, LANES), lambda h: (h, 0, 0)),
        out_shape=shape_of((heads, owned * BLOCK, LANES), BF16),
        scratch_shapes=[pltpu.VMEM((owned * BLOCK, LANES), I32)],
        compiler_params=params(),
        cost_estimate=cost(heads * 4.0 * slots * tokens * LANES, 4e6),
        name="unpack_q",
    )(index, q_recv)

    token_rows = None
    for (first, count_heads), recv in zip(splits, received, strict=True):
        reply = pl.pallas_call(
            functools.partial(attend_kernel, first=first),
            grid_spec=pltpu.PrefetchScalarGridSpec(
                num_scalar_prefetch=1,
                grid=(count_heads,),
                in_specs=[
                    pl.BlockSpec((1, owned, BLOCK), lambda h, fetch, first=first: (h + first, 0, 0)),
                    pl.BlockSpec(
                        (1, owned * BLOCK, LANES), lambda h, fetch, first=first: (h + first, 0, 0)
                    ),
                    pl.BlockSpec(
                        (groups, 1, KCAP, BLOCK, 2 * LANES), lambda h, fetch: (0, h, 0, 0, 0)
                    ),
                ],
                out_specs=pl.BlockSpec((groups, 1, capacity, LANES), lambda h, fetch: (0, h, 0, 0)),
                scratch_shapes=[pltpu.VMEM((owned * BLOCK, LANES), BF16)],
            ),
            out_shape=shape_of((groups, count_heads, capacity, LANES), BF16),
            compiler_params=params(),
            cost_estimate=cost(
                count_heads * 4.0 * owned * BLOCK * PAIRS * BLOCK * LANES,
                count_heads * 6e6,
                count_heads * owned * BLOCK * PAIRS * BLOCK,
            ),
            name=f"attend_{first}",
        )(fetch, index, q_sorted, recv)
        returned = exchange(reply, "seq")
        operands = (slot, returned) + (() if token_rows is None else (token_rows,))
        token_rows = pl.pallas_call(
            final_kernel,
            grid=(count_heads,),
            in_specs=[
                pl.BlockSpec((1, chunks, LANES), lambda h, first=first: (h + first, 0, 0)),
                pl.BlockSpec((groups, 1, capacity, LANES), lambda h: (0, h, 0, 0)),
            ]
            + [pl.BlockSpec(memory_space=pl.ANY)] * (len(operands) - 2),
            out_specs=pl.BlockSpec((parts, part, LANES), lambda h, first=first: (0, 0, h + first)),
            out_shape=shape_of((parts, part, width), BF16),
            scratch_shapes=[pltpu.VMEM((tokens, LANES), I32)],
            input_output_aliases={} if token_rows is None else {2: 0},
            compiler_params=params(),
            cost_estimate=cost(count_heads * 4.0 * slots * tokens * LANES, 2e6),
            name=f"final_{first}",
        )(*operands)
    rows = exchange(token_rows, "head")
    return rows.transpose(1, 0, 2).reshape(part, parts * width)


def solution(mesh):
    in_specs = (
        P(("seq", "head"), None),
        P(("seq", "head"), None),
        P(("seq", "head"), None),
        P("head", "seq"),
        P("head", "seq"),
        P("head", None, None),
    )
    out_specs = P(("seq", "head"), None)
    return jax.shard_map(
        per_device, mesh=mesh, in_specs=in_specs, out_specs=out_specs, check_vma=False
    )
```

```python
import functools
import math

import jax
import jax.numpy as jnp
from jax import lax
from jax.experimental import pallas as pl
from jax.experimental.pallas import tpu as pltpu
from jax.sharding import PartitionSpec as P

BLOCK = 128
PAIRS = 16
KCAP = 4
LANES = 128
META = 16
VMEM_LIMIT = 56 * 1024 * 1024
BF16 = jnp.bfloat16
F32 = jnp.float32
I32 = jnp.int32


def dot(left, right):
    return jnp.dot(left, right, preferred_element_type=F32)


def iota(shape, dim):
    return lax.broadcasted_iota(I32, shape, dim)


def params():
    return pltpu.CompilerParams(vmem_limit_bytes=VMEM_LIMIT)


def slot_kernel(ids_ref, slot_ref, count_ref, *, groups, owned, capacity):
    clusters = groups * owned
    chunks = ids_ref.shape[1]
    row = iota((clusters, LANES), 0)
    lane = iota((clusters, LANES), 1)
    before = iota((LANES, 2 * LANES), 0)
    after = iota((LANES, 2 * LANES), 1)
    running = ((after >= LANES) | (before <= after)).astype(BF16)
    every = jnp.ones((LANES, LANES), BF16)
    counts = jnp.zeros((clusters, LANES), F32)
    for chunk in range(chunks):
        hit = (ids_ref[0, chunk : chunk + 1, :] == row).astype(BF16)
        counts = counts + dot(hit, every)
    first = iota((clusters, clusters), 0)
    second = iota((clusters, clusters), 1)
    inside = ((second < first) & (second // owned == first // owned)).astype(BF16)
    carry = dot(inside, counts.astype(BF16)) + ((row // owned) * capacity - 1).astype(F32)
    own = jnp.where(lane == row % owned, counts, 0.0).astype(BF16)
    of_group = (iota((groups, clusters), 0) == iota((groups, clusters), 1) // owned).astype(BF16)
    count_ref[0] = dot(of_group, own)
    for chunk in range(chunks):
        match = ids_ref[0, chunk : chunk + 1, :] == row
        sums = dot(match.astype(BF16), running)
        picked = jnp.where(match, sums[:, :LANES] + carry, 0.0)
        slot_ref[0, chunk : chunk + 1, :] = jnp.sum(picked, axis=0, keepdims=True).astype(I32)
        carry = carry + sums[:, LANES:]


def spread(index, rows, store, slots, step):
    flat = jnp.concatenate([index[i : i + 1, :] for i in range(index.shape[0])], axis=1)
    count = flat.shape[1]
    within = iota((step, count), 0)

    def body(i, carry):
        onehot = (flat - i * step == within).astype(BF16)
        store(i, dot(onehot, rows).astype(BF16))
        return carry

    lax.fori_loop(0, slots // step, body, 0)


def collect(index, packed, wide_ref, store, step):
    turned = index.astype(F32).T
    chunks = index.shape[0]
    for i in range(chunks):
        wide_ref[i * LANES : (i + 1) * LANES, :] = jnp.broadcast_to(
            turned[:, i : i + 1], (LANES, LANES)
        ).astype(I32)
    lane = iota((step, LANES), 1)
    narrow = packed.shape[1] == LANES
    depth = packed.shape[0] // 2 if narrow else packed.shape[0]
    if narrow:
        packed = jnp.concatenate([packed[:depth], packed[depth:]], axis=1)

    def body(i, carry):
        wide = wide_ref[pl.ds(pl.multiple_of(i * step, step), step), :]
        second = wide >= depth
        if narrow:
            wide = jnp.where(second, wide - depth, wide)
        wide = wide - lane
        onehot = jnp.concatenate(
            [(wide == t * LANES).astype(BF16) for t in range(depth // LANES)], axis=1
        )
        block = dot(onehot, packed)
        if narrow:
            block = jnp.where(second, block[:, LANES:], block[:, :LANES])
        store(i, block.astype(BF16))
        return carry

    lax.fori_loop(0, chunks * LANES // step, body, 0)


def split_kernel(key_ref, value_ref, out_ref):
    parts, _, _, width = out_ref.shape
    stride = key_ref.shape[1] // parts
    for part in range(parts):
        columns = slice(part * stride, part * stride + width)
        out_ref[part, 0] = key_ref[:, columns]
        out_ref[part, 1] = value_ref[:, columns]


def split_rest_kernel(me_ref, key_ref, value_ref, query_ref, *out_refs):
    parts = len(out_refs) // 2
    stride = key_ref.shape[1] // parts
    me = me_ref[0]
    for k in range(parts):
        start = jnp.bitwise_xor(me, k) * stride
        last = pl.ds(pl.multiple_of(start + stride - LANES, LANES), LANES)
        out_refs[k][0] = key_ref[:, last]
        out_refs[k][1] = value_ref[:, last]
        out_refs[parts + k][...] = query_ref[:, pl.ds(pl.multiple_of(start, LANES), stride)]


def partner_order(me, index, parts):
    each = index.shape[0] // parts
    row = iota(index.shape, 0)
    rows = []
    for k in range(parts):
        for j in range(each):
            wanted = jnp.bitwise_xor(me, k) * each + j
            rows.append(jnp.sum(jnp.where(row == wanted, index, 0), axis=0, keepdims=True))
    return jnp.concatenate(rows, axis=0)


def pack_kv_kernel(slot_ref, count_ref, key_ref, value_ref, out_ref):
    head = pl.program_id(0)
    heads = pl.num_programs(0)
    groups, rows, _ = out_ref.shape
    of_heads = count_ref.shape[0] // 2
    capacity = (rows - META) // (of_heads - 1)
    tokens = key_ref.shape[0] * key_ref.shape[2]
    keys = key_ref[:, 0].reshape(tokens, LANES)
    values = value_ref[:, 0].reshape(tokens, LANES)
    at = pl.ds(pl.multiple_of(head * capacity, META), capacity)
    per = groups // 2

    def store(i, block):
        out_ref[pl.ds(per * i, per), at, :] = block.reshape(per, capacity, 2 * LANES)

    both = jnp.concatenate([keys, values], axis=1)
    spread(slot_ref[0], both, store, groups * capacity, per * capacity)

    @pl.when(head == heads - 1)
    def _():
        row = iota((groups, META, LANES), 1)
        for side in range(2):
            block = jnp.zeros((groups, META, LANES), F32)
            for h in range(of_heads):
                counts = count_ref[(1 - side) * of_heads + h]
                block = jnp.where(row == h, counts[:, None, :], block)
            out_ref[:, rows - META :, side * LANES : (side + 1) * LANES] = block.astype(BF16)


def pack_last_kernel(me_ref, slot_ref, *refs):
    *part_refs, out_ref = refs
    groups, capacity, _ = out_ref.shape
    index = partner_order(me_ref[0], slot_ref[0], len(part_refs))
    keys = jnp.concatenate([ref[0] for ref in part_refs], axis=0)
    values = jnp.concatenate([ref[1] for ref in part_refs], axis=0)
    per = groups // 2

    def store(i, block):
        out_ref[pl.ds(per * i, per)] = block.reshape(per, capacity, 2 * LANES)

    both = jnp.concatenate([keys, values], axis=1)
    spread(index, both, store, groups * capacity, per * capacity)


def pack_q_kernel(me_ref, slot_ref, *refs):
    *part_refs, out_ref = refs
    groups, _, capacity, _ = out_ref.shape
    index = partner_order(me_ref[0], slot_ref[0], len(part_refs))
    queries = jnp.concatenate([ref[...] for ref in part_refs], axis=0)
    per = groups // 2

    def store(i, block):
        out_ref[pl.ds(per * i, per), 0] = block.reshape(per, capacity, LANES)

    spread(index, queries, store, groups * capacity, per * capacity)


def sources(counts, capacity):
    groups = counts.shape[0]
    padded = jnp.concatenate([counts, jnp.zeros((LANES - groups, LANES), F32)], axis=0).astype(BF16)
    row = iota((LANES, LANES), 0)
    col = iota((LANES, LANES), 1)
    below = dot((col < row).astype(BF16), padded)
    offset = dot(padded, (row < col).astype(BF16))
    start = (row * capacity).astype(F32) + offset - below
    below_t = below.T[:groups]
    start_t = start.T[:groups]
    place = iota((groups, LANES), 1).astype(F32)
    found = jnp.broadcast_to(start_t[:, 0:1], (groups, LANES))
    for source in range(1, groups):
        found = jnp.where(below_t[:, source : source + 1] <= place, start_t[:, source : source + 1], found)
    return (found + place).astype(I32)


def unpack_kv_kernel(
    pick_ref,
    in_ref,
    last_in_ref,
    meta_ref,
    first_ref,
    last_ref,
    query_source_ref,
    wide_ref,
    sorted_ref,
):
    head = pl.program_id(0)
    heads = pl.num_programs(0)
    groups, capacity, _ = in_ref.shape
    row = iota(meta_ref.shape, 1)
    counts = jnp.sum(jnp.where(row == head, meta_ref[...].astype(F32), 0.0), axis=1)
    query_source_ref[0] = sources(counts[:, LANES:], capacity)
    key_source = sources(counts[:, :LANES], capacity)

    def store(i, block):
        sorted_ref[pl.ds(8 * i, 8)] = block.reshape(8, BLOCK, 2 * LANES)

    def send(packed_ref, out_ref):
        packed = packed_ref[...].reshape(groups * capacity, 2 * LANES)
        collect(key_source, packed, wide_ref, store, 8 * BLOCK)

        def copy(i, carry):
            for j in range(KCAP):
                out_ref[i, 0, j] = sorted_ref[pick_ref[head, i, j]]
            return carry

        lax.fori_loop(0, groups, copy, 0)

    @pl.when(head < heads - 1)
    def _():
        send(in_ref, first_ref)

    @pl.when(head == heads - 1)
    def _():
        send(last_in_ref, last_ref)


def unpack_q_kernel(index_ref, in_ref, out_ref, wide_ref):
    groups, _, capacity, _ = in_ref.shape
    packed = in_ref[:, 0].reshape(groups * capacity, LANES)
    step = 8 * BLOCK

    def store(i, block):
        out_ref[0, pl.ds(pl.multiple_of(i * step, step), step), :] = block

    collect(index_ref[0], packed, wide_ref, store, step)


def final_kernel(index_ref, in_ref, *refs):
    out_ref, wide_ref = refs[-2:]
    groups, _, capacity, _ = in_ref.shape
    packed = in_ref[:, 0].reshape(groups * capacity, LANES)
    part = out_ref.shape[1]

    def store(i, block):
        out_ref[pl.ds(4 * i, 4)] = block.reshape(4, part, LANES)

    collect(index_ref[0], packed, wide_ref, store, 4 * part)


def attend_kernel(fetch_ref, index_ref, query_ref, recv_ref, out_ref, attended_ref, *, first):
    head = pl.program_id(0) + first
    groups, _, capacity, _ = out_ref.shape
    owned = query_ref.shape[1] // BLOCK
    scale = math.log2(math.e) / math.sqrt(LANES)

    def one(cluster):
        rows = pl.ds(pl.multiple_of(cluster * BLOCK, BLOCK), BLOCK)
        queries = query_ref[0, rows, :]
        blocks = []
        for pair in range(PAIRS):
            at = fetch_ref[head, cluster, pair]
            blocks.append((at // KCAP, at % KCAP))
        keys = jnp.concatenate([recv_ref[b, 0, j, :, :LANES] for b, j in blocks], axis=0)
        values = jnp.concatenate([recv_ref[b, 0, j, :, LANES:] for b, j in blocks], axis=0)
        scores = lax.dot_general(
            queries, keys, (((1,), (1,)), ((), ())), preferred_element_type=F32
        )
        weights = jnp.exp2((scores - jnp.max(scores, axis=1, keepdims=True)) * scale)
        total = jnp.sum(weights, axis=1, keepdims=True)
        mixed = dot(weights.astype(BF16), values)
        attended_ref[rows, :] = (mixed / total).astype(BF16)

    def body(i, carry):
        for j in range(4):
            one(4 * i + j)
        return carry

    lax.fori_loop(0, owned // 4, body, 0)

    per = groups // 2

    def store(i, block):
        out_ref[pl.ds(per * i, per), 0] = block.reshape(per, capacity, LANES)

    spread(index_ref[0], attended_ref[...], store, groups * capacity, per * capacity)


def shape_of(shape, dtype):
    return jax.ShapeDtypeStruct(shape, dtype)


def cost(flops, moved, exps=0):
    return pl.CostEstimate(flops=int(flops), bytes_accessed=int(moved), transcendentals=int(exps))


def exchange(array, axis):
    return lax.all_to_all(array, axis, split_axis=0, concat_axis=0, tiled=True)


def tables(cluster_pairs, my_index, groups):
    heads, clusters, _ = cluster_pairs.shape
    owned = clusters // groups
    by_group = cluster_pairs.reshape(heads, groups, owned * PAIRS)
    local = jnp.arange(owned, dtype=I32)
    earlier = (local[:, None] < local[None, :]).astype(F32)
    needed = jnp.any(by_group[:, :, None, :] == (my_index * owned + local)[None, None, :, None], axis=3)
    order = jnp.einsum("hac,cd->had", needed.astype(F32), earlier).astype(I32)
    hits = needed[:, :, None, :] & (order[:, :, None, :] == jnp.arange(KCAP, dtype=I32)[:, None])
    pick = jnp.sum(jnp.where(hits, local, 0), axis=3)
    own = lax.dynamic_index_in_dim(by_group, my_index, 1, keepdims=False)
    every = jnp.arange(clusters, dtype=I32)
    same = own[:, :, None] == every
    wanted = jnp.any(same, axis=1).reshape(heads, groups, owned)
    rank = jnp.einsum("hac,cd->had", wanted.astype(F32), earlier).astype(I32)
    position = (rank + jnp.arange(groups, dtype=I32)[None, :, None] * KCAP).reshape(heads, 1, clusters)
    fetch = jnp.sum(jnp.where(same, position, 0), axis=2)
    return pick, fetch.reshape(heads, owned, PAIRS)


def per_device(query_rows, key_rows, value_rows, query_cluster, key_cluster, cluster_pairs):
    heads, tokens = query_cluster.shape
    groups = lax.axis_size("seq")
    parts = lax.axis_size("head")
    my_index = lax.axis_index("seq")
    clusters = cluster_pairs.shape[1]
    owned = clusters // groups
    capacity = 3 * tokens // (2 * groups)
    slots = groups * capacity
    part = tokens // parts
    width = heads * LANES
    chunks = tokens // LANES

    most = heads - 1
    me = lax.axis_index("head").astype(I32).reshape(1)

    kv_sent = pl.pallas_call(
        split_kernel,
        grid=(8,),
        in_specs=[pl.BlockSpec((part // 8, parts * width), lambda i: (i, 0))] * 2,
        out_specs=pl.BlockSpec((parts, 2, part // 8, most * LANES), lambda i: (0, 0, i, 0)),
        out_shape=shape_of((parts, 2, part, most * LANES), BF16),
        compiler_params=params(),
        cost_estimate=cost(0, 6e6),
        name="split_kv",
    )(key_rows, value_rows)
    kv_tok = exchange(kv_sent, "head")
    last_parts = [shape_of((2, part, LANES), BF16)] * parts
    query_parts = [shape_of((part, width), BF16)] * parts
    pieces = pl.pallas_call(
        split_rest_kernel,
        grid_spec=pltpu.PrefetchScalarGridSpec(
            num_scalar_prefetch=1,
            grid=(2,),
            in_specs=[pl.BlockSpec((part // 2, parts * width), lambda i, me: (i, 0))] * 3,
            out_specs=[pl.BlockSpec((2, part // 2, LANES), lambda i, me: (0, i, 0))] * parts
            + [pl.BlockSpec((part // 2, width), lambda i, me: (i, 0))] * parts,
        ),
        out_shape=last_parts + query_parts,
        compiler_params=params(),
        cost_estimate=cost(0, 6e6),
        name="split_rest",
    )(me, key_rows, value_rows, query_rows)
    ids = jnp.concatenate([query_cluster, key_cluster], axis=0).reshape(2 * heads, chunks, LANES)
    slot, count = pl.pallas_call(
        functools.partial(slot_kernel, groups=groups, owned=owned, capacity=capacity),
        grid=(2 * heads,),
        in_specs=[pl.BlockSpec((1, chunks, LANES), lambda h: (h, 0, 0))],
        out_specs=[
            pl.BlockSpec((1, chunks, LANES), lambda h: (h, 0, 0)),
            pl.BlockSpec((1, groups, LANES), lambda h: (h, 0, 0)),
        ],
        out_shape=[
            shape_of((2 * heads, chunks, LANES), I32),
            shape_of((2 * heads, groups, LANES), F32),
        ],
        compiler_params=params(),
        cost_estimate=cost(2e9 * heads, 1e6),
        name="slots",
    )(ids)
    pick, fetch = tables(cluster_pairs, my_index, groups)

    *pieces, kv_tok = lax.optimization_barrier((*pieces, kv_tok))
    kv_packed = pl.pallas_call(
        pack_kv_kernel,
        grid=(most,),
        in_specs=[
            pl.BlockSpec((1, chunks, LANES), lambda h: (h + heads, 0, 0)),
            pl.BlockSpec((2 * heads, groups, LANES), lambda h: (0, 0, 0)),
            pl.BlockSpec((parts, 1, part, LANES), lambda h: (0, 0, 0, h)),
            pl.BlockSpec((parts, 1, part, LANES), lambda h: (0, 1, 0, h)),
        ],
        out_specs=pl.BlockSpec((groups, most * capacity + META, 2 * LANES), lambda h: (0, 0, 0)),
        out_shape=shape_of((groups, most * capacity + META, 2 * LANES), BF16),
        compiler_params=params(),
        cost_estimate=cost(most * 4.0 * slots * tokens * LANES, 8e6),
        name="pack_kv",
    )(slot, count, kv_tok, kv_tok)
    kv_recv = exchange(kv_packed, "seq")

    def to_partner(array, k):
        return lax.ppermute(array, "head", [(i, i ^ k) for i in range(parts)])

    *pieces, _ = lax.optimization_barrier((*pieces, kv_packed))
    last_tok = [to_partner(piece, k) if k else piece for k, piece in enumerate(pieces[:parts])]
    both = lax.optimization_barrier((*last_tok, *pieces[parts:]))
    last_tok, q_sent = both[:parts], both[parts:]
    q_tok = [to_partner(piece, k) if k else piece for k, piece in enumerate(q_sent)]

    last_packed = pl.pallas_call(
        pack_last_kernel,
        grid_spec=pltpu.PrefetchScalarGridSpec(
            num_scalar_prefetch=1,
            grid=(1,),
            in_specs=[pl.BlockSpec((1, chunks, LANES), lambda i, me: (2 * heads - 1, 0, 0))]
            + [pl.BlockSpec((2, part, LANES), lambda i, me: (0, 0, 0))] * parts,
            out_specs=pl.BlockSpec((groups, capacity, 2 * LANES), lambda i, me: (0, 0, 0)),
        ),
        out_shape=shape_of((groups, capacity, 2 * LANES), BF16),
        compiler_params=params(),
        cost_estimate=cost(4.0 * slots * tokens * LANES, 3e6),
        name="pack_last",
    )(me, slot, *last_tok)
    last_packed, kv_recv, *q_tok = lax.optimization_barrier((last_packed, kv_recv, *q_tok))
    last_kv_recv = exchange(last_packed, "seq")

    q_packed = pl.pallas_call(
        pack_q_kernel,
        grid_spec=pltpu.PrefetchScalarGridSpec(
            num_scalar_prefetch=1,
            grid=(heads,),
            in_specs=[pl.BlockSpec((1, chunks, LANES), lambda h, me: (h, 0, 0))]
            + [pl.BlockSpec((part, LANES), lambda h, me: (0, h))] * parts,
            out_specs=pl.BlockSpec((groups, 1, capacity, LANES), lambda h, me: (0, h, 0, 0)),
        ),
        out_shape=shape_of((groups, heads, capacity, LANES), BF16),
        compiler_params=params(),
        cost_estimate=cost(heads * 4.0 * slots * tokens * LANES, 4e6),
        name="pack_q",
    )(me, slot, *q_tok)
    q_packed, last_kv_recv = lax.optimization_barrier((q_packed, last_kv_recv))
    q_recv = exchange(q_packed, "seq")

    splits = ((0, heads - 1), (heads - 1, 1))
    block = (groups, 1, KCAP, BLOCK, 2 * LANES)
    first_sent, last_sent, index = pl.pallas_call(
        unpack_kv_kernel,
        grid_spec=pltpu.PrefetchScalarGridSpec(
            num_scalar_prefetch=1,
            grid=(heads,),
            in_specs=[
                pl.BlockSpec(
                    (groups, capacity, 2 * LANES), lambda h, pick: (0, jnp.minimum(h, most - 1), 0)
                ),
                pl.BlockSpec((groups, capacity, 2 * LANES), lambda h, pick: (0, 0, 0)),
                pl.BlockSpec(
                    (groups, META, 2 * LANES), lambda h, pick: (0, most * capacity // META, 0)
                ),
            ],
            out_specs=[
                pl.BlockSpec(block, lambda h, pick: (0, jnp.minimum(h, heads - 2), 0, 0, 0)),
                pl.BlockSpec(block, lambda h, pick: (0, 0, 0, 0, 0)),
                pl.BlockSpec((1, owned, BLOCK), lambda h, pick: (h, 0, 0)),
            ],
            scratch_shapes=[
                pltpu.VMEM((owned * BLOCK, LANES), I32),
                pltpu.VMEM((owned, BLOCK, 2 * LANES), BF16),
            ],
        ),
        out_shape=[
            shape_of((groups, heads - 1, KCAP, BLOCK, 2 * LANES), BF16),
            shape_of(block, BF16),
            shape_of((heads, owned, BLOCK), I32),
        ],
        compiler_params=params(),
        cost_estimate=cost(heads * 4.0 * slots * tokens * LANES, heads * 6e6),
        name="unpack_kv",
    )(pick, kv_recv, last_kv_recv, kv_recv)
    first_recv = exchange(first_sent, "seq")
    last_recv = exchange(last_sent, "seq")
    received = (first_recv, last_recv)
    q_recv, index, _ = lax.optimization_barrier((q_recv, index, first_recv))

    q_sorted = pl.pallas_call(
        unpack_q_kernel,
        grid=(heads,),
        in_specs=[
            pl.BlockSpec((1, owned, BLOCK), lambda h: (h, 0, 0)),
            pl.BlockSpec((groups, 1, capacity, LANES), lambda h: (0, h, 0, 0)),
        ],
        out_specs=pl.BlockSpec((1, owned * BLOCK, LANES), lambda h: (h, 0, 0)),
        out_shape=shape_of((heads, owned * BLOCK, LANES), BF16),
        scratch_shapes=[pltpu.VMEM((owned * BLOCK, LANES), I32)],
        compiler_params=params(),
        cost_estimate=cost(heads * 4.0 * slots * tokens * LANES, 4e6),
        name="unpack_q",
    )(index, q_recv)

    token_rows = None
    for (first, count_heads), recv in zip(splits, received, strict=True):
        reply = pl.pallas_call(
            functools.partial(attend_kernel, first=first),
            grid_spec=pltpu.PrefetchScalarGridSpec(
                num_scalar_prefetch=1,
                grid=(count_heads,),
                in_specs=[
                    pl.BlockSpec((1, owned, BLOCK), lambda h, fetch, first=first: (h + first, 0, 0)),
                    pl.BlockSpec(
                        (1, owned * BLOCK, LANES), lambda h, fetch, first=first: (h + first, 0, 0)
                    ),
                    pl.BlockSpec(
                        (groups, 1, KCAP, BLOCK, 2 * LANES), lambda h, fetch: (0, h, 0, 0, 0)
                    ),
                ],
                out_specs=pl.BlockSpec((groups, 1, capacity, LANES), lambda h, fetch: (0, h, 0, 0)),
                scratch_shapes=[pltpu.VMEM((owned * BLOCK, LANES), BF16)],
            ),
            out_shape=shape_of((groups, count_heads, capacity, LANES), BF16),
            compiler_params=params(),
            cost_estimate=cost(
                count_heads * 4.0 * owned * BLOCK * PAIRS * BLOCK * LANES,
                count_heads * 6e6,
                count_heads * owned * BLOCK * PAIRS * BLOCK,
            ),
            name=f"attend_{first}",
        )(fetch, index, q_sorted, recv)
        returned = exchange(reply, "seq")
        operands = (slot, returned) + (() if token_rows is None else (token_rows,))
        token_rows = pl.pallas_call(
            final_kernel,
            grid=(count_heads,),
            in_specs=[
                pl.BlockSpec((1, chunks, LANES), lambda h, first=first: (h + first, 0, 0)),
                pl.BlockSpec((groups, 1, capacity, LANES), lambda h: (0, h, 0, 0)),
            ]
            + [pl.BlockSpec(memory_space=pl.ANY)] * (len(operands) - 2),
            out_specs=pl.BlockSpec((parts, part, LANES), lambda h, first=first: (0, 0, h + first)),
            out_shape=shape_of((parts, part, width), BF16),
            scratch_shapes=[pltpu.VMEM((tokens, LANES), I32)],
            input_output_aliases={} if token_rows is None else {2: 0},
            compiler_params=params(),
            cost_estimate=cost(count_heads * 4.0 * slots * tokens * LANES, 2e6),
            name=f"final_{first}",
        )(*operands)
    rows = exchange(token_rows, "head")
    return rows.transpose(1, 0, 2).reshape(part, parts * width)


def solution(mesh):
    in_specs = (
        P(("seq", "head"), None),
        P(("seq", "head"), None),
        P(("seq", "head"), None),
        P("head", "seq"),
        P("head", "seq"),
        P("head", None, None),
    )
    out_specs = P(("seq", "head"), None)
    return jax.shard_map(
        per_device, mesh=mesh, in_specs=in_specs, out_specs=out_specs, check_vma=False
    )
```
